32 devices in a mesh: dp: 8 (over y, x, core), tensor: 4 (over z).
Axes of the slice: x: 2, y: 2, z: 4, core: 2. Of those that a mesh axis runs over, the one named last changes fastest.
Arguments:
- tokens: bfloat16 [16384, 768], P(('dp', 'tensor')), may hold values from -6 to 6
- cotangent: bfloat16 [16384, 768], P(('dp', 'tensor')), may hold values from -6 to 6
- patch_count: int32 [64], P('dp'), may hold values from 100 to 216
- word_mask: int32 [64, 40], P('dp'), may hold values 0 or 1
- norm1_gain: float32 [768], replicated, may hold values from 0.1 to 1.9
- norm1_shift: float32 [768], replicated, may hold values from -1.5 to 1.5
- query_weight: bfloat16 [768, 768], P(None, 'tensor'), may hold values from -0.21875 to 0.21875
- query_bias: float32 [768], P('tensor'), may hold values from -1.5 to 1.5
- key_weight: bfloat16 [768, 768], P(None, 'tensor'), may hold values from -0.21875 to 0.21875
- value_weight: bfloat16 [768, 768], P(None, 'tensor'), may hold values from -0.21875 to 0.21875
- value_bias: float32 [768], P('tensor'), may hold values from -1.5 to 1.5
- out_weight: bfloat16 [768, 768], P('tensor'), may hold values from -0.875 to 0.875
- out_bias: float32 [768], replicated, may hold values from -1.5 to 1.5
- norm2_gain: float32 [768], replicated, may hold values from 0.1 to 1.9
- norm2_shift: float32 [768], replicated, may hold values from -1.5 to 1.5
- up_weight: bfloat16 [768, 3072], P(None, 'tensor'), may hold values from -0.21875 to 0.21875
- up_bias: float32 [3072], P('tensor'), may hold values from -1.5 to 1.5
- down_weight: bfloat16 [3072, 768], P('tensor'), may hold values from -0.109375 to 0.109375
- down_bias: float32 [768], replicated, may hold values from -1.5 to 1.5
Outputs:
- layer_out: bfloat16 [16384, 768], P(('dp', 'tensor'))
- input_grad: float32 [16384, 768], P(('dp', 'tensor'))
- norm1_gain_grad: float32 [768], replicated
- norm1_shift_grad: float32 [768], replicated
- query_weight_grad: float32 [768, 768], P(None, 'tensor')
- query_bias_grad: float32 [768], P('tensor')
- key_weight_grad: float32 [768, 768], P(None, 'tensor')
- value_weight_grad: float32 [768, 768], P(None, 'tensor')
- value_bias_grad: float32 [768], P('tensor')
- out_weight_grad: float32 [768, 768], P('tensor')
- out_bias_grad: float32 [768], replicated
- norm2_gain_grad: float32 [768], replicated
- norm2_shift_grad: float32 [768], replicated
- up_weight_grad: float32 [768, 3072], P(None, 'tensor')
- up_bias_grad: float32 [3072], P('tensor')
- down_weight_grad: float32 [3072, 768], P('tensor')
- down_bias_grad: float32 [768], replicated
The draws below stay inside these ranges and needn't reach their ends.
All inputs are finite; a program needn't handle non-finite values. No bound on the sum of `word_mask` on one device may be relied on, other than what follows from the above.
Results may differ from the reference program's by a relative error of at most 0.019.
Values may be sent and summed in bfloat16 or wider, within the bound.
No kernel may reach another device: no remote copies, remote signals or barrier semaphores. Data moves between devices by JAX's collectives and lax.ppermute only.
A program may use at most 128 MiB of HBM per device.

```python
import math
import jax
import jax.numpy as jnp
from jax import lax

D = 768
HEADS = 12
HEAD_DIM = 64
FF = 3072
WORDS = 40
PATCHES = 216
SLOTS = 256
ITEMS = 64
TOKENS = 16384


def set_ends(values, rng, low, largest):
    shape = values.shape
    place = [jax.random.randint(jax.random.fold_in(rng, axis), (), 0, shape[axis]) for axis in range(len(shape))]
    values = values.at[tuple(place)].set(low)
    longest = shape.index(max(shape))
    place[longest] = (place[longest] + 1) % shape[longest]
    return values.at[tuple(place)].set(largest)


def block_levels(stream_key, extent, split, low, high):
    def one(axis_at, shards_of):
        heights = jax.random.uniform(jax.random.fold_in(jax.random.fold_in(stream_key, 6), axis_at), (shards_of,), jnp.float32, low / len(split), high / len(split))
        return jnp.repeat(jnp.exp(heights), extent[axis_at] // shards_of).reshape((-1,) + (1,) * (len(extent) - axis_at - 1))

    factor_of = one(*split[0])
    for cut in split[1:]:
        factor_of = factor_of * one(*cut)
    return factor_of


def bell_draw(key, extent, width, most, pieces=(), held_as=jnp.bfloat16):
    loudness = block_levels(key, extent, pieces, -0.22, 0.18) if pieces else 1.0
    values = jax.random.normal(key, extent, jnp.float32) * width * loudness
    return jnp.minimum(jnp.maximum(values, -most), most).astype(held_as)


def setup_inputs(seed: int = 0) -> dict:
    key_list = jax.random.split(jax.random.key(seed), 20)
    tokens = bell_draw(key_list[0], (TOKENS, D), 1.0, 6.0, ((0, 32),))
    cotangent = bell_draw(key_list[1], (TOKENS, D), 1.0, 6.0, ((0, 32),))
    patch_count = set_ends(jax.random.randint(key_list[2], (ITEMS,), PATCHES * 100 // 216, PATCHES + 1), jax.random.fold_in(key_list[2], 1), PATCHES * 100 // 216, PATCHES).astype(jnp.int32)
    word_mask = set_ends((jax.random.randint(key_list[3], (ITEMS, WORDS), 0, 4) < 3).astype(jnp.int32), jax.random.fold_in(key_list[3], 1), 0, 1)
    norm1_gain = jnp.clip(1.0 + 0.18 * jax.random.normal(key_list[4], (D,), jnp.float32), 0.1, 1.9)
    norm1_shift = bell_draw(key_list[5], (D,), 0.3, 1.5, (), jnp.float32)
    query_weight = bell_draw(key_list[6], (D, D), D ** -0.5, 0.21875, ((1, 4),))
    query_bias = bell_draw(key_list[7], (D,), 0.3, 1.5, ((0, 4),), jnp.float32)
    key_weight = bell_draw(key_list[8], (D, D), D ** -0.5, 0.21875, ((1, 4),))
    value_weight = bell_draw(key_list[9], (D, D), D ** -0.5, 0.21875, ((1, 4),))
    value_bias = bell_draw(key_list[10], (D,), 0.3, 1.5, ((0, 4),), jnp.float32)
    out_weight = bell_draw(key_list[11], (D, D), (D // 16) ** -0.5, 0.875, ((0, 4),))
    out_bias = bell_draw(key_list[12], (D,), 0.3, 1.5, (), jnp.float32)
    norm2_gain = jnp.clip(1.0 + 0.18 * jax.random.normal(key_list[13], (D,), jnp.float32), 0.1, 1.9)
    norm2_shift = bell_draw(key_list[14], (D,), 0.3, 1.5, (), jnp.float32)
    up_weight = bell_draw(key_list[15], (D, FF), D ** -0.5, 0.21875, ((1, 4),))
    up_bias = bell_draw(key_list[16], (FF,), 0.3, 1.5, ((0, 4),), jnp.float32)
    down_weight = bell_draw(key_list[17], (FF, D), FF ** -0.5, 0.109375, ((0, 4),))
    down_bias = bell_draw(key_list[18], (D,), 0.3, 1.5, (), jnp.float32)
    return {"tokens": tokens, "cotangent": cotangent, "patch_count": patch_count, "word_mask": word_mask, "norm1_gain": norm1_gain, "norm1_shift": norm1_shift, "query_weight": query_weight, "query_bias": query_bias, "key_weight": key_weight, "value_weight": value_weight, "value_bias": value_bias, "out_weight": out_weight, "out_bias": out_bias, "norm2_gain": norm2_gain, "norm2_shift": norm2_shift, "up_weight": up_weight, "up_bias": up_bias, "down_weight": down_weight, "down_bias": down_bias}


@jax.custom_vjp
def low(v):
    return lax.optimization_barrier(v.astype(jnp.bfloat16)).astype(jnp.float32)

@jax.custom_vjp
def low_back(v):
    return v

def low_keep(v):
    return (low(v), None)

def low_pass(kept, grad):
    return (grad,)

def back_keep(v):
    return (v, None)

def back_low(kept, grad):
    return (low(grad),)
low.defvjp(low_keep, low_pass)
low_back.defvjp(back_keep, back_low)
PRECISE = lax.Precision.HIGHEST
NORM_EPS = 1e-05
MASKED = -1e+30

def matmul(left, right):
    return jnp.dot(left, right, precision=PRECISE)

def norm_rows(values, gain, shift):
    row_mean = lax.optimization_barrier(jnp.mean(values, axis=-1, keepdims=True))
    centered = values - row_mean
    variance = lax.optimization_barrier(jnp.mean(centered * centered, axis=-1, keepdims=True))
    return centered * lax.rsqrt(variance + NORM_EPS) * gain + shift

def key_valid(patch_count, word_mask):
    patch_slot = jnp.arange(PATCHES, dtype=jnp.int32)
    patch_live = patch_slot[None, :] < patch_count[:, None]
    return jnp.concatenate([word_mask > 0, patch_live], axis=1)

def attend(inputs):
    queries, keyset, values, valid_keys = inputs
    raw_scores = jnp.einsum('qhe,khe->hqk', queries, keyset, precision=PRECISE) * HEAD_DIM ** (-0.5)
    scores = jnp.where(valid_keys[None, None, :], low_back(raw_scores), MASKED)
    row_max = lax.optimization_barrier(jnp.max(scores, axis=-1, keepdims=True))
    exp_scores = jnp.exp(scores - row_max)
    attn_probs = exp_scores / lax.optimization_barrier(jnp.sum(exp_scores, axis=-1, keepdims=True))
    return jnp.einsum('hqk,khe->qhe', low(attn_probs), values, precision=PRECISE)

def layer_block(tokens_block, valid_block, params):
    norm1_gain, norm1_shift, query_weight, query_bias, key_weight, value_weight, value_bias, out_weight, out_bias, norm2_gain, norm2_shift, up_weight, up_bias, down_weight, down_bias = params
    item_count = valid_block.shape[0]
    normed1 = low(norm_rows(tokens_block, norm1_gain, norm1_shift))
    queries = low_back(low(matmul(normed1, query_weight) + query_bias))
    keyset = low_back(low(matmul(normed1, key_weight)))
    values = low_back(low(matmul(normed1, value_weight) + value_bias))
    head_shape = (item_count, SLOTS, HEADS, HEAD_DIM)
    context = lax.map(jax.checkpoint(attend), (queries.reshape(head_shape), keyset.reshape(head_shape), values.reshape(head_shape), valid_block))
    context = low_back(low(context.reshape(item_count * SLOTS, D)))
    middle = tokens_block + low_back(matmul(context, out_weight) + out_bias)
    normed2 = low(norm_rows(middle, norm2_gain, norm2_shift))
    hidden_pre = low_back(matmul(normed2, up_weight) + up_bias)
    hidden_act = low(jax.nn.gelu(hidden_pre, approximate=False))
    return middle + matmul(hidden_act, down_weight) + down_bias

def reference(tokens, cotangent, patch_count, word_mask, norm1_gain, norm1_shift, query_weight, query_bias, key_weight, value_weight, value_bias, out_weight, out_bias, norm2_gain, norm2_shift, up_weight, up_bias, down_weight, down_bias):
    params = tuple((param.astype(jnp.float32) for param in (norm1_gain, norm1_shift, query_weight, query_bias, key_weight, value_weight, value_bias, out_weight, out_bias, norm2_gain, norm2_shift, up_weight, up_bias, down_weight, down_bias)))
    valid_keys = key_valid(patch_count, word_mask)
    block_items = math.gcd(ITEMS, max(1, 4096 // SLOTS))
    block_count = ITEMS // block_items
    block_tokens = tokens.astype(jnp.float32).reshape(block_count, block_items * SLOTS, D)
    block_grads = cotangent.astype(jnp.float32).reshape(block_count, block_items * SLOTS, D)
    block_valid = valid_keys.reshape(block_count, block_items, SLOTS)

    def block_step(totals, inputs):
        rows_in, grads_in, valid_in = inputs

        def forward(rows_value, param_set):
            return layer_block(rows_value, valid_in, param_set)
        result, pullback = jax.vjp(forward, rows_in, params)
        rows_grad, param_grads = pullback(grads_in)
        totals = jax.tree.map(lambda running, update: running + update, totals, param_grads)
        return (totals, (result.astype(jnp.bfloat16), rows_grad))
    zero_grads = tuple((jnp.zeros_like(param) for param in params))
    totals, (outputs, input_grads) = lax.scan(block_step, zero_grads, (block_tokens, block_grads, block_valid))
    return (outputs.reshape(TOKENS, D), input_grads.reshape(TOKENS, D), totals[0], totals[1], totals[2], totals[3], totals[4], totals[5], totals[6], totals[7], totals[8], totals[9], totals[10], totals[11], totals[12], totals[13], totals[14])
```

```python
import functools

import jax
import jax.numpy as jnp
from jax import lax
from jax.experimental import pallas as pl
from jax.experimental.pallas import tpu as pltpu
from jax.sharding import PartitionSpec as P

D = 768
HEAD_DIM = 64
WORDS = 40
SLOTS = 256
NORM_EPS = 1e-05
MASKED = -1e30
BLOCK = 8
PIECE = D // BLOCK
F32 = jnp.float32
BF16 = jnp.bfloat16
VMEM_LIMIT = 56 * 1024 * 1024


def nn(left, right):
    return lax.dot_general(left, right, (((1,), (0,)), ((), ())), preferred_element_type=F32)


def nt(left, right):
    return lax.dot_general(left, right, (((1,), (1,)), ((), ())), preferred_element_type=F32)


def tn(left, right):
    return lax.dot_general(left, right, (((0,), (0,)), ((), ())), preferred_element_type=F32)


def norm_stats(values):
    mean = jnp.mean(values, axis=-1, keepdims=True)
    centered = values - mean
    factor = lax.rsqrt(jnp.mean(centered * centered, axis=-1, keepdims=True) + NORM_EPS)
    return centered * factor, factor


def norm_back(normed, factor, gain, grad):
    scaled = grad * gain
    mean_scaled = jnp.mean(scaled, axis=-1, keepdims=True)
    mean_product = jnp.mean(scaled * normed, axis=-1, keepdims=True)
    return factor * (scaled - mean_scaled - normed * mean_product)


def column_sum(values):
    return jnp.sum(values, axis=0, keepdims=True)


def flat(size):
    return jax.ShapeDtypeStruct(size, F32)


def half(size):
    return jax.ShapeDtypeStruct(size, BF16)


def vmem():
    return pl.BlockSpec(memory_space=pltpu.VMEM)


def smem():
    return pl.BlockSpec(memory_space=pltpu.SMEM)


def anywhere():
    return pl.BlockSpec(memory_space=pl.ANY)


def call(body, outs, in_specs, args, scratch=(), flops=0, moved=0):
    return pl.pallas_call(
        body,
        out_shape=outs,
        in_specs=in_specs,
        out_specs=jax.tree.map(lambda _: vmem(), outs),
        scratch_shapes=list(scratch),
        compiler_params=pltpu.CompilerParams(vmem_limit_bytes=VMEM_LIMIT),
        cost_estimate=pl.CostEstimate(flops=int(flops), bytes_accessed=int(moved), transcendentals=0),
    )(*args)


def fetch(place, pieces, target, sems):
    me = place[0]
    copies = []
    for slot, (ref, index) in enumerate(pieces):
        row = pl.multiple_of((me ^ slot) * PIECE, PIECE)
        copies.append(
            pltpu.make_async_copy(ref.at[index], target.at[pl.ds(row, PIECE)], sems.at[slot])
        )
    for copy in copies:
        copy.start()
    return copies


def deliver(place, whole, send_ref, keep_ref):
    me = place[0]
    for slot in range(BLOCK):
        row = pl.multiple_of((me ^ slot) * PIECE, PIECE)
        ref = send_ref if slot % 2 else keep_ref
        ref[slot // 2] = whole[pl.ds(row, PIECE), :]


def norm1_kernel(tokens_ref, gain_ref, shift_ref, h1_ref):
    normed, _ = norm_stats(tokens_ref[...].astype(F32))
    h1_ref[...] = (normed * gain_ref[...] + shift_ref[...]).astype(BF16)


def head_views(block, low):
    lane = lax.broadcasted_iota(jnp.int32, block.shape, 1)
    inside = lane < HEAD_DIM if low else lane >= HEAD_DIM
    return jnp.where(inside, block, jnp.zeros_like(block))


def attend_body(shift_ref, h1_ref, bias_ref, weight_ref, proj_ref, context_ref, lse_ref):
    h1 = h1_ref[...]
    bias = bias_ref[...]
    first = nn(h1, weight_ref[:, 0:512]) + bias[:, 0:512]
    lane = lax.broadcasted_iota(jnp.int32, (1, 512), 1)
    is_query = (lane < 128) | ((lane >= 384) & (lane < 448))
    first = first * jnp.where(is_query, HEAD_DIM**-0.5, 1.0)
    proj_ref[:, 0:512] = first.astype(BF16)
    proj_ref[:, 512:640] = (nn(h1, weight_ref[:, 640:768]) + bias[:, 512:640]).astype(BF16)
    for item in range(h1.shape[0] // SLOTS):
        rows = pl.ds(item * SLOTS, SLOTS)
        shift = shift_ref[:, item : item + 1]
        pair = jnp.zeros((SLOTS, 128), F32)
        for head in range(3):
            if head < 2:
                query = head_views(proj_ref[rows, 0:128], head == 0)
                key = proj_ref[rows, 128:256]
                value = head_views(proj_ref[rows, 256:384], head == 0)
            else:
                query = proj_ref[rows, 384:448]
                key = proj_ref[rows, 448:512]
                value = proj_ref[rows, 576:640]
            scores = nt(key, query) + shift
            top = jnp.max(scores, axis=0, keepdims=True)
            exps = jnp.exp(scores - top)
            total = jnp.sum(exps, axis=0, keepdims=True)
            probs = (exps * (1.0 / total)).astype(BF16)
            lse_ref[item * 3 + head : item * 3 + head + 1, :] = top + jnp.log(total)
            part = tn(probs, value)
            if head < 2:
                pair = pair + part
            else:
                context_ref[rows, 128:256] = jnp.concatenate(
                    [part, jnp.zeros((SLOTS, 64), F32)], axis=1
                ).astype(BF16)
        context_ref[rows, 0:128] = pair.astype(BF16)


def attend(shard, place, shift, h1, bias, own_weight, pieces):
    rows = h1.shape[0]
    outs = (half((rows, 640)), half((rows, 256)), flat((3 * rows // SLOTS, SLOTS)))
    if shard == 0:
        def body(place_ref, shift_ref, h1_ref, bias_ref, weight_ref, *out_refs):
            attend_body(shift_ref, h1_ref, bias_ref, weight_ref, *out_refs)

        return call(body, outs, [smem()] + [vmem()] * 4, (place, shift, h1, bias, own_weight),
                    flops=2e9, moved=1e6)

    def body(place_ref, shift_ref, h1_ref, bias_ref, *refs):
        weight_ref, sems = refs[-2:]
        for copy in fetch(place_ref, [(ref, shard - 1) for ref in refs[:8]], weight_ref, sems):
            copy.wait()
        attend_body(shift_ref, h1_ref, bias_ref, weight_ref, *refs[8:11])

    return call(body, outs, [smem()] + [vmem()] * 3 + [anywhere()] * 8,
                (place, shift, h1, bias, *pieces),
                scratch=[pltpu.VMEM((D, D), BF16), pltpu.SemaphoreType.DMA((8,))],
                flops=2e9, moved=1e6)


def middle_kernel(place, tokens_ref, out_bias_ref, gain_ref, shift_ref, own_ref, *refs):
    contexts, pieces = refs[:4], refs[4:12]
    middle_ref, h2_ref, weight_ref, sems = refs[12:]
    for shard in range(1, 4):
        for copy in fetch(place, [(ref, shard - 1) for ref in pieces], weight_ref.at[shard - 1], sems.at[shard - 1]):
            pass
    total = tokens_ref[...].astype(F32) + out_bias_ref[...]
    total = total + nt(contexts[0][...], own_ref[:, 512:768])
    for shard in range(1, 4):
        for slot, ref in enumerate(pieces):
            row = pl.multiple_of((place[0] ^ slot) * PIECE, PIECE)
            pltpu.make_async_copy(
                ref.at[shard - 1], weight_ref.at[shard - 1, pl.ds(row, PIECE)], sems.at[shard - 1, slot]
            ).wait()
        total = total + nt(contexts[shard][...], weight_ref[shard - 1, :, 512:768])
    middle_ref[...] = total
    normed, _ = norm_stats(total)
    h2_ref[...] = (normed * gain_ref[...] + shift_ref[...]).astype(BF16)


def up_kernel(shard, place, h2_ref, grad_ref, bias_ref, *refs):
    if shard == 0:
        weight_ref, act_ref, slope_ref, send_ref, keep_ref, whole = refs
    else:
        act_ref, slope_ref, send_ref, keep_ref, whole, weight_ref, sems = refs[8:]
        for copy in fetch(place, [(ref, shard - 1) for ref in refs[:8]], weight_ref, sems):
            copy.wait()
    h2 = h2_ref[...]
    for start in range(0, D, 256):
        cols = pl.ds(start, 256)
        pre = nn(h2, weight_ref[:, cols]) + bias_ref[:, cols]
        below = 0.5 * (1.0 + lax.erf(pre * (2.0**-0.5)))
        act = (pre * below).astype(BF16)
        act_ref[:, cols] = act
        slope_ref[:, cols] = below + pre * (jnp.exp(-0.5 * pre * pre) * ((2.0 * jnp.pi) ** -0.5))
        whole[cols, :] = tn(act, grad_ref[...]).astype(BF16)
    deliver(place, whole, send_ref, keep_ref)


def up(shard, place, h2, grad, bias, own_weight, pieces):
    rows = h2.shape[0]
    outs = (half((rows, D)), flat((rows, D)), half((4, PIECE, D)), half((4, PIECE, D)))
    scratch = [pltpu.VMEM((D, D), BF16)]
    if shard == 0:
        return call(functools.partial(up_kernel, shard), outs, [smem()] + [vmem()] * 4,
                    (place, h2, grad, bias, own_weight), scratch=scratch, flops=3e9, moved=1e6)
    return call(functools.partial(up_kernel, shard), outs, [smem()] + [vmem()] * 3 + [anywhere()] * 8,
                (place, h2, grad, bias, *pieces),
                scratch=scratch + [pltpu.VMEM((D, D), BF16), pltpu.SemaphoreType.DMA((8,))],
                flops=3e9, moved=1e6)


def down_kernel(shard, place, h2_ref, grad_ref, slope_ref, *refs):
    if shard == 0:
        weight_ref, dpre_ref, sums_ref, send_ref, keep_ref, whole = refs
    else:
        dpre_ref, sums_ref, send_ref, keep_ref, whole, weight_ref, sems = refs[8:]
        for copy in fetch(place, [(ref, shard - 1) for ref in refs[:8]], weight_ref, sems):
            copy.wait()
    grad = grad_ref[...]
    for start in range(0, D, 256):
        cols = pl.ds(start, 256)
        dpre = (nt(grad, weight_ref[cols, :]) * slope_ref[:, cols]).astype(BF16)
        dpre_ref[:, cols] = dpre
        sums_ref[:, cols] = column_sum(dpre.astype(F32))
    whole[...] = tn(h2_ref[...], dpre_ref[...]).astype(BF16)
    deliver(place, whole, send_ref, keep_ref)


def down(shard, place, h2, grad, slope, own_weight, pieces):
    rows = h2.shape[0]
    outs = (half((rows, D)), flat((1, D)), half((4, PIECE, D)), half((4, PIECE, D)))
    scratch = [pltpu.VMEM((D, D), BF16)]
    if shard == 0:
        return call(functools.partial(down_kernel, shard), outs, [smem()] + [vmem()] * 4,
                    (place, h2, grad, slope, own_weight), scratch=scratch, flops=2e9, moved=1e6)
    return call(functools.partial(down_kernel, shard), outs, [smem()] + [vmem()] * 3 + [anywhere()] * 8,
                (place, h2, grad, slope, *pieces),
                scratch=scratch + [pltpu.VMEM((D, D), BF16), pltpu.SemaphoreType.DMA((8,))],
                flops=2e9, moved=1e6)


def fetch_all(place, pieces, weight_ref, sems):
    return [
        fetch(place, [(ref, shard - 1) for ref in pieces], weight_ref.at[shard - 1], sems.at[shard - 1])
        for shard in range(1, 4)
    ]


def norm2_back_kernel(place, middle_ref, grad_ref, gain_ref, own_ref, *refs):
    dpres, pieces = refs[:4], refs[4:12]
    dmid_ref, rounded_ref, sums_ref, weight_ref, sems = refs[12:]
    copies = fetch_all(place, pieces, weight_ref, sems)
    total = nt(dpres[0][...], own_ref[...])
    for shard in range(1, 4):
        for copy in copies[shard - 1]:
            copy.wait()
        total = total + nt(dpres[shard][...], weight_ref[shard - 1])
    normed, factor = norm_stats(middle_ref[...])
    grad = grad_ref[...].astype(F32)
    dmid = grad + norm_back(normed, factor, gain_ref[...], total)
    rounded = dmid.astype(BF16)
    dmid_ref[...] = dmid
    rounded_ref[...] = rounded
    sums_ref[0:1, :] = column_sum(rounded.astype(F32))
    sums_ref[1:2, :] = column_sum(total * normed)
    sums_ref[2:3, :] = column_sum(total)
    sums_ref[3:4, :] = column_sum(grad)


def attend_back_kernel(shard, place, shift_ref, dmid_ref, h1_ref, proj_ref, context_ref, lse_ref, *refs):
    if shard == 0:
        weight_ref, dproj_ref, sums_ref, send_ref, keep_ref, whole = refs
    else:
        dproj_ref, sums_ref, send_ref, keep_ref, whole, weight_ref, sems = refs[8:]
        for copy in fetch(place, [(ref, shard - 1) for ref in refs[:8]], weight_ref, sems):
            copy.wait()
    dmid = dmid_ref[...]
    dcontext = nn(dmid, weight_ref[:, 512:768]).astype(BF16)
    scale = HEAD_DIM**-0.5
    for item in range(dmid.shape[0] // SLOTS):
        rows = pl.ds(item * SLOTS, SLOTS)
        low = item * SLOTS
        shift = shift_ref[:, item : item + 1]
        pairs = [jnp.zeros((SLOTS, 128), F32)] * 3
        for head in range(3):
            if head < 2:
                query = head_views(proj_ref[rows, 0:128], head == 0)
                key = proj_ref[rows, 128:256]
                masked_key = head_views(key, head == 0)
                value = proj_ref[rows, 256:384]
                dctx = head_views(dcontext[low : low + SLOTS, 0:128], head == 0)
            else:
                query = proj_ref[rows, 384:448]
                key = proj_ref[rows, 448:512]
                masked_key = key
                value = proj_ref[rows, 576:640]
                dctx = dcontext[low : low + SLOTS, 128:192]
            lse = lse_ref[item * 3 + head : item * 3 + head + 1, :]
            probs = jnp.exp(nt(key, query) + shift - lse)
            dvalue = nn(probs.astype(BF16), dctx)
            dprobs = nt(value, dctx)
            delta = jnp.sum(probs * dprobs, axis=0, keepdims=True)
            dscores = (probs * (dprobs - delta)).astype(BF16)
            dkey = nn(dscores, query)
            dquery = tn(dscores, masked_key) * scale
            if head < 2:
                pairs = [a + b for a, b in zip(pairs, (dquery, dkey, dvalue))]
            else:
                dproj_ref[rows, 384:512] = jnp.concatenate([dquery, dkey], axis=1).astype(BF16)
                dproj_ref[rows, 512:640] = jnp.concatenate(
                    [jnp.zeros((SLOTS, 64), F32), dvalue], axis=1
                ).astype(BF16)
        for index, value in enumerate(pairs):
            dproj_ref[rows, index * 128 : (index + 1) * 128] = value.astype(BF16)
    sums_ref[...] = jnp.zeros(sums_ref.shape, F32)
    sums_ref[:, 0:640] = column_sum(dproj_ref[...].astype(F32))
    h1 = h1_ref[...]
    whole[:, 0:512] = tn(h1, dproj_ref[:, 0:512]).astype(BF16)
    whole[:, 512:640] = tn(dmid, context_ref[:, 0:128]).astype(BF16)
    whole[:, 640:768] = (tn(dmid, context_ref[:, 128:256]) + tn(h1, dproj_ref[:, 512:640])).astype(BF16)
    deliver(place, whole, send_ref, keep_ref)


def attend_back(shard, place, shift, dmid, h1, proj, context, lse, own_weight, pieces):
    rows = h1.shape[0]
    outs = (half((rows, 640)), flat((1, D)), half((4, PIECE, D)), half((4, PIECE, D)))
    scratch = [pltpu.VMEM((D, D), BF16)]
    first = (place, shift, dmid, h1, proj, context, lse)
    if shard == 0:
        return call(functools.partial(attend_back_kernel, shard), outs, [smem()] + [vmem()] * 7,
                    (*first, own_weight), scratch=scratch, flops=3e9, moved=1e6)
    return call(functools.partial(attend_back_kernel, shard), outs, [smem()] + [vmem()] * 6 + [anywhere()] * 8,
                (*first, *pieces),
                scratch=scratch + [pltpu.VMEM((D, D), BF16), pltpu.SemaphoreType.DMA((8,))],
                flops=3e9, moved=1e6)


def norm1_back_kernel(place, tokens_ref, dmid_ref, gain_ref, own_ref, *refs):
    dprojs, pieces = refs[:4], refs[4:12]
    out_ref, sums_ref, weight_ref, sems = refs[12:]
    copies = fetch_all(place, pieces, weight_ref, sems)
    total = nt(dprojs[0][:, 0:512], own_ref[:, 0:512]) + nt(dprojs[0][:, 512:640], own_ref[:, 640:768])
    for shard in range(1, 4):
        for copy in copies[shard - 1]:
            copy.wait()
        total = total + nt(dprojs[shard][:, 0:512], weight_ref[shard - 1, :, 0:512])
        total = total + nt(dprojs[shard][:, 512:640], weight_ref[shard - 1, :, 640:768])
    normed, factor = norm_stats(tokens_ref[...].astype(F32))
    out_ref[...] = dmid_ref[...] + norm_back(normed, factor, gain_ref[...], total)
    sums_ref[0:1, :] = column_sum(total * normed)
    sums_ref[1:2, :] = column_sum(total)


def layer_out_kernel(place, middle_ref, bias_ref, own_ref, *refs):
    acts, pieces = refs[:4], refs[4:12]
    out_ref, weight_ref, sems = refs[12:]
    copies = fetch_all(place, pieces, weight_ref, sems)
    total = middle_ref[...] + bias_ref[...] + nn(acts[0][...], own_ref[...])
    for shard in range(1, 4):
        for copy in copies[shard - 1]:
            copy.wait()
        total = total + nn(acts[shard][...], weight_ref[shard - 1])
    out_ref[...] = total.astype(BF16)


WEIGHTS = (pltpu.VMEM((3, D, D), BF16), pltpu.SemaphoreType.DMA((3, 8)))


def add_kernel(first_keep, first_got, second_keep, second_got, send_ref, keep_ref):
    send_ref[...] = (first_keep[...].astype(F32) + first_got[...].astype(F32)).astype(BF16)
    keep_ref[...] = (second_keep[...].astype(F32) + second_got[...].astype(F32)).astype(BF16)


def add_split(keep, got, dim, stride):
    count = keep.shape[dim] // 2
    other = keep.shape[1 - dim]
    shape = list(keep.shape)
    shape[dim] = count

    def index(bit):
        def of(outer, inner):
            at = (inner // stride) * 2 * stride + inner % stride + bit * stride
            place = [outer, outer]
            place[dim] = at
            return (place[0], place[1], 0, 0)

        return of

    def out_index(outer, inner):
        place = [outer, outer]
        place[dim] = inner
        return (place[0], place[1], 0, 0)

    block = (1, 1, PIECE, D)
    return pl.pallas_call(
        add_kernel,
        grid=(other, count),
        out_shape=(half(tuple(shape)), half(tuple(shape))),
        in_specs=[pl.BlockSpec(block, index(1))] * 2 + [pl.BlockSpec(block, index(0))] * 2,
        out_specs=(pl.BlockSpec(block, out_index), pl.BlockSpec(block, out_index)),
        compiler_params=pltpu.CompilerParams(vmem_limit_bytes=VMEM_LIMIT),
        cost_estimate=pl.CostEstimate(flops=0, bytes_accessed=3 * keep.size * 2, transcendentals=0),
    )(keep, got, keep, got)


def first_add_kernel(bit, *refs):
    send_ref, keep_ref = refs[8:]
    for shard in range(4):
        keep, got = refs[shard], refs[4 + shard]
        counts = [0, 0]
        for slot in range(4):
            value = (keep[slot].astype(F32) + got[slot].astype(F32)).astype(BF16)
            chosen = slot // bit % 2
            (send_ref if chosen else keep_ref)[shard, counts[chosen]] = value
            counts[chosen] += 1


def slots_of(first):
    other = 6 - first
    order = {0: (0, 0), other: (0, 1), 1: (1, 0), other + 1: (1, 1)}
    order.update({first: (2, 0), 6: (2, 1), first + 1: (3, 0), 7: (3, 1)})
    return order


def finish_plain_kernel(first, place, *refs):
    out_ref = refs[4]
    for slot, (array, index) in slots_of(first).items():
        out_ref[place[0] ^ slot] = refs[array][index].astype(F32)


def finish_heads_kernel(first, place, *refs):
    query_ref, key_ref, value_ref, out_ref, whole = refs[4:]
    for slot, (array, index) in slots_of(first).items():
        row = pl.multiple_of((place[0] ^ slot) * PIECE, PIECE)
        whole[pl.ds(row, PIECE), :] = refs[array][index].astype(F32)
    query_ref[:, 0:128] = whole[:, 0:128]
    query_ref[:, 128:192] = whole[:, 384:448]
    key_ref[:, 0:128] = whole[:, 128:256]
    key_ref[:, 128:192] = whole[:, 448:512]
    value_ref[:, 0:128] = whole[:, 256:384]
    value_ref[:, 128:192] = whole[:, 704:768]
    out_ref[...] = whole[:, 512:704].T


def shards(dp_size, z_size, tokens, cotangent, patch_count, word_mask, norm1_gain, norm1_shift, query_weight,
           query_bias, key_weight, value_weight, value_bias, out_weight, out_bias, norm2_gain, norm2_shift,
           up_weight, up_bias, down_weight, down_bias):
    rows = tokens.shape[0]
    items = rows // SLOTS
    me = lax.axis_index("dp") % BLOCK
    place = me.reshape(1).astype(jnp.int32)

    def swap(value, bit):
        return lax.ppermute(value, "dp", [(i, i ^ bit) for i in range(dp_size)])

    def swap_z(value, bit):
        return lax.ppermute(value, "tensor", [(i, i ^ bit) for i in range(z_size)])

    def row(vector):
        return vector.reshape(1, -1)

    first_item = lax.axis_index("tensor") * items
    counts = lax.dynamic_slice(patch_count, (first_item,), (items,))
    words = lax.dynamic_slice(word_mask, (first_item, 0), (items, WORDS))
    patch_slot = jnp.arange(SLOTS - WORDS, dtype=jnp.int32)
    valid = jnp.concatenate([words > 0, patch_slot[None, :] < counts[:, None]], axis=1)
    shift = jnp.where(valid, 0.0, MASKED).astype(F32).T

    out_t = out_weight.T
    attn_own = jnp.concatenate(
        [query_weight[:, :128], key_weight[:, :128], value_weight[:, :128], query_weight[:, 128:],
         key_weight[:, 128:], out_t, value_weight[:, 128:]], axis=1)
    zeros = jnp.zeros((128,), F32)
    bias_own = row(jnp.concatenate(
        [query_bias[:128], zeros, value_bias[:128], query_bias[128:], zeros, value_bias[128:], up_bias]))

    bias2 = swap_z(bias_own, 2)
    bias13 = swap_z(jnp.concatenate([bias_own, bias2], axis=0), 1)
    biases = [bias_own, bias13[0:1], bias2, bias13[1:2]]

    def spread(own):
        piece = lax.dynamic_slice(own.reshape(BLOCK, PIECE, D), (me, 0, 0), (1, PIECE, D))
        from1 = swap_z(piece, 1)
        from2 = swap_z(piece, 2)
        from3 = swap_z(from2, 1)
        mine = jnp.concatenate([from1, from2, from3], axis=0)
        near = [mine, swap(mine, 2), swap(mine, 4), swap(mine, 6)]
        far = [swap(value, 1) for value in near]
        return [part for pair in zip(near, far) for part in pair]

    attn_pieces = spread(attn_own)
    up_pieces = spread(up_weight)
    down_pieces = spread(down_weight)

    h1 = call(norm1_kernel, half((rows, D)), [vmem()] * 3, (tokens, row(norm1_gain), row(norm1_shift)),
              flops=1e9)
    proj, context, lse = zip(*[
        attend(t, place, shift, h1, biases[t][:, 0:640], attn_own, attn_pieces) for t in range(4)])
    middle, h2 = call(
        middle_kernel, (flat((rows, D)), half((rows, D))),
        [smem()] + [vmem()] * 9 + [anywhere()] * 8,
        (place, tokens, row(out_bias), row(norm2_gain), row(norm2_shift), attn_own, *context, *attn_pieces),
        scratch=WEIGHTS, flops=2e9)
    act, slope, down_send, down_keep = zip(*[
        up(t, place, h2, cotangent, biases[t][:, 640:], up_weight, up_pieces) for t in range(4)])

    def reduce(send, keep, bit):
        got = [swap(value, 1) for value in send]
        both = call(functools.partial(first_add_kernel, bit // 2),
                    (half((4, 2, PIECE, D)), half((4, 2, PIECE, D))), [vmem()] * 8, (*keep, *got), moved=15e6)
        travel, stay = both
        travel, stay = add_split(stay, swap(travel, bit), 0, 1)
        travel, stay = add_split(stay, swap_z(travel, 1), 0, 1)
        stay = add_pair(stay, swap_z(travel, 2))
        other = 6 - bit
        stay = add_swapped(stay, swap(stay, other))
        if dp_size > BLOCK:
            groups = [list(range(i, dp_size, BLOCK)) for i in range(BLOCK)]
            stay = lax.psum(stay, "dp", axis_index_groups=groups)
        beside = swap(stay, bit)
        return [stay, swap(stay, 1), beside, swap(beside, 1)]

    def add_pair(keep, got):
        return (keep.astype(F32) + got.astype(F32)).astype(BF16)[0]

    def add_swapped(keep, got):
        return (keep.astype(F32) + got[::-1].astype(F32)).astype(BF16)

    down_sum = reduce(down_send, down_keep, 2)

    dpre, up_sums, up_send, up_keep = zip(*[
        down(t, place, h2, cotangent, slope[t], down_weight, down_pieces) for t in range(4)])
    up_sum = reduce(up_send, up_keep, 4)

    dmid, dmid_b, mid_sums = call(
        norm2_back_kernel, (flat((rows, D)), half((rows, D)), flat((4, D))),
        [smem()] + [vmem()] * 8 + [anywhere()] * 8,
        (place, middle, cotangent, row(norm2_gain), up_weight, *dpre, *up_pieces),
        scratch=WEIGHTS, flops=4e9)

    dproj, head_sums, attn_send, attn_keep = zip(*[
        attend_back(t, place, shift, dmid_b, h1, proj[t], context[t], lse[t], attn_own, attn_pieces)
        for t in range(4)])
    attn_sum = reduce(attn_send, attn_keep, 2)

    input_grad, in_sums = call(
        norm1_back_kernel, (flat((rows, D)), flat((2, D))),
        [smem()] + [vmem()] * 8 + [anywhere()] * 8,
        (place, tokens, dmid, row(norm1_gain), attn_own, *dproj, *attn_pieces),
        scratch=WEIGHTS, flops=4e9)
    layer_out = call(
        layer_out_kernel, half((rows, D)), [smem()] + [vmem()] * 7 + [anywhere()] * 8,
        (place, middle, row(down_bias), down_weight, *act, *down_pieces), scratch=WEIGHTS, flops=4e9)

    small = jnp.concatenate([in_sums, mid_sums, *up_sums, *head_sums, jnp.zeros((2, D), F32)], axis=0)

    def turned(value, bit):
        parts = [value[:6]] + [value[low + (t ^ bit)][None] for low in (6, 10) for t in range(4)] + [value[14:]]
        return jnp.concatenate(parts, axis=0)

    for bit in (1, 2, 4):
        small = small + swap(small, bit)
    if dp_size > BLOCK:
        groups = [list(range(i, dp_size, BLOCK)) for i in range(BLOCK)]
        small = lax.psum(small, "dp", axis_index_groups=groups)
    for bit in (1, 2):
        small = small + turned(swap_z(small, bit), bit)

    def finish(quads, first):
        return call(functools.partial(finish_plain_kernel, first), flat((BLOCK, PIECE, D)),
                    [smem()] + [vmem()] * 4, (place, *quads), moved=4e6).reshape(D, D)

    down_weight_grad = finish(down_sum, 2)
    up_weight_grad = finish(up_sum, 4)
    heads = (flat((D, 192)), flat((D, 192)), flat((D, 192)), flat((192, D)))
    query_weight_grad, key_weight_grad, value_weight_grad, out_weight_grad = call(
        functools.partial(finish_heads_kernel, 2), heads, [smem()] + [vmem()] * 4, (place, *attn_sum),
        scratch=[pltpu.VMEM((D, D), F32)], moved=4e6)
    head = small[10]
    return (
        layer_out, input_grad, small[0], small[1], query_weight_grad,
        jnp.concatenate([head[0:128], head[384:448]]), key_weight_grad, value_weight_grad,
        jnp.concatenate([head[256:384], head[576:640]]), out_weight_grad, small[2], small[3], small[4],
        up_weight_grad, small[6], down_weight_grad, small[5],
    )


def solution(mesh):
    rows = P(("dp", "tensor"), None)
    columns = P(None, "tensor")
    part = P("tensor")
    part_rows = P("tensor", None)
    whole = P()
    return jax.shard_map(
        functools.partial(shards, mesh.shape["dp"], mesh.shape["tensor"]),
        mesh=mesh,
        in_specs=(rows, rows, P("dp"), P("dp", None), whole, whole, columns, part, columns, columns, part,
                  part_rows, whole, whole, whole, columns, part, part_rows, whole),
        out_specs=(rows, rows, whole, whole, columns, part, columns, columns, part, part_rows, whole, whole,
                   whole, columns, part, part_rows, whole),
        check_vma=False,
    )
```

```python
import functools
import math

import jax
import jax.numpy as jnp
from jax import lax
from jax.experimental import pallas as pl
from jax.experimental.pallas import tpu as pltpu
from jax.sharding import PartitionSpec as P

D = 768
HEAD_DIM = 64
HEADS_OWN = 3
ITEMS_OWN = 2
WORDS = 40
SLOTS = 256
NORM_EPS = 1e-05
MASKED = -1e30
BLOCK = 8
PIECE = D // BLOCK
SUB = PIECE // 2
F32 = jnp.float32
BF16 = jnp.bfloat16
STACK = 6 * 1024 * 1024


def nn(left, right):
    return lax.dot_general(left, right, (((1,), (0,)), ((), ())), preferred_element_type=F32)


def nt(left, right):
    return lax.dot_general(left, right, (((1,), (1,)), ((), ())), preferred_element_type=F32)


def tn(left, right):
    return lax.dot_general(left, right, (((0,), (0,)), ((), ())), preferred_element_type=F32)


def norm_stats(values):
    mean = jnp.mean(values, axis=-1, keepdims=True)
    centered = values - mean
    factor = lax.rsqrt(jnp.mean(centered * centered, axis=-1, keepdims=True) + NORM_EPS)
    return centered * factor, factor


def norm_back(normed, factor, gain, grad):
    scaled = grad * gain
    mean_scaled = jnp.mean(scaled, axis=-1, keepdims=True)
    mean_product = jnp.mean(scaled * normed, axis=-1, keepdims=True)
    return factor * (scaled - mean_scaled - normed * mean_product)


def column_sum(values):
    return jnp.sum(values, axis=0, keepdims=True)


def row_sum(values):
    return jnp.sum(values, axis=1, keepdims=True)


def flat(*size):
    return jax.ShapeDtypeStruct(size, F32)


def half(*size):
    return jax.ShapeDtypeStruct(size, BF16)


def size_of(shape, dtype):
    shape = (1,) * (2 - len(shape)) + tuple(shape)
    return math.prod(shape[:-2]) * -(-shape[-2] // 8) * 8 * -(-shape[-1] // 128) * 128 * jnp.dtype(dtype).itemsize


class Chain:
    def __init__(self):
        self.last = None

    def tie(self, value):
        return value if self.last is None else lax.optimization_barrier((value, self.last))[0]

    def __call__(self, body, outs, *args, scratch=(), scalars=1):
        args = args[:scalars] + (self.tie(args[scalars]),) + args[scalars + 1 :]
        got = kernel(body, outs, *args, scratch=scratch, scalars=scalars)
        self.last = jax.tree.leaves(got)[-1]
        return got


def kernel(body, outs, *args, scratch=(), scalars=1):
    held = list(args[scalars:]) + jax.tree.leaves(outs) + list(scratch)
    limit = STACK + sum(size_of(h.shape, h.dtype) for h in held)
    return pl.pallas_call(
        body,
        name=(body.func if isinstance(body, functools.partial) else body).__name__,
        out_shape=outs,
        in_specs=[pl.BlockSpec(memory_space=pltpu.SMEM)] * scalars
        + [pl.BlockSpec(memory_space=pltpu.VMEM)] * (len(args) - scalars),
        out_specs=jax.tree.map(lambda _: pl.BlockSpec(memory_space=pltpu.VMEM), outs),
        scratch_shapes=[pltpu.VMEM(s.shape, s.dtype) for s in scratch],
        compiler_params=pltpu.CompilerParams(vmem_limit_bytes=limit),
        cost_estimate=pl.CostEstimate(flops=1, bytes_accessed=1, transcendentals=1),
    )(*args)


def line(ref):
    return ref[...].reshape(1, -1)


def row_of(me, core, part, near, side):
    mine, x, y = me & 1, (me >> 1) & 1, me >> 2
    ahead, beside = (x, y) if part == 0 else (y, x)
    row = part * (D // 2) + ((ahead ^ near) * 2 + (mine ^ core)) * PIECE + (beside ^ side) * SUB
    return pl.multiple_of(row, 16)


PLACES = [(core, part, near, side) for core in (0, 1) for part in (0, 1) for near in (0, 1) for side in (0, 1)]


def heads_prep_kernel(place, query_ref, key_ref, value_ref, out_ref, whole_ref, piece_ref):
    for index, ref in enumerate((query_ref, key_ref, value_ref, out_ref)):
        whole_ref[index * 192 : index * 192 + 192, :] = ref[...]
    piece_ref[...] = whole_ref[pl.ds(pl.multiple_of(place[0] * PIECE, 16), PIECE), :]


def hidden_prep_kernel(which, place, weight_ref, *refs):
    if which == 0:
        order_ref, piece_ref, scratch = refs
        scratch[...] = weight_ref[...].T
        weight_ref = scratch
    else:
        before_ref, order_ref, piece_ref = refs
        piece_ref[0] = before_ref[0]
    for index, (core, part, near, side) in enumerate(PLACES):
        block = weight_ref[pl.ds(row_of(place[0], core, part, near, side), SUB), :]
        order_ref[index * SUB : (index + 1) * SUB, :] = block
        if core + near + side == 0:
            piece_ref[which, part * SUB : (part + 1) * SUB, :] = block


def small_prep_kernel(place, counts, words_ref, up_bias_ref, query_bias_ref, value_bias_ref, bias_ref, shift_ref,
                      column_ref, keys_ref):
    bias_ref[...] = jnp.zeros(bias_ref.shape, F32)
    for first, ref in ((0, up_bias_ref), (D, query_bias_ref), (D + 192, value_bias_ref)):
        size = ref.shape[0]
        column_ref[first : first + size, :] = jnp.broadcast_to(line(ref), (8, size)).T
    for index, spot in enumerate(PLACES):
        bias_ref[:, index : index + 1] = column_ref[pl.ds(row_of(place[0], *spot), SUB), 0:1]
    for index in range(8):
        low = D + index * SUB
        bias_ref[:, 16 + index : 17 + index] = column_ref[low : low + SUB, 0:1]
    lane = lax.broadcasted_iota(jnp.int32, (1, SLOTS), 1)
    keys_ref[...] = jnp.zeros(keys_ref.shape, F32)
    for item in range(ITEMS_OWN):
        at = place[1] * ITEMS_OWN + item
        keys_ref[item : item + 1, 0:WORDS] = words_ref[pl.ds(at, 1), :].astype(F32)
        live = jnp.where(lane < WORDS, keys_ref[item : item + 1, :], jnp.where(lane - WORDS < counts[at], 1.0, 0.0))
        keys_ref[item : item + 1, :] = jnp.where(live > 0, 0.0, MASKED)
    shift_ref[...] = keys_ref[...].T


def pack_kernel(place, *refs):
    for index, ref in enumerate(refs[:-1]):
        refs[-1][index] = ref[...]


def pack_heads_kernel(place, *refs):
    for index, ref in enumerate(refs[:-1]):
        refs[-1][:, index] = ref[...]


def split_kernel(place, *refs):
    for shard in range(3):
        for kind in range(2):
            for part in range(2):
                refs[3 + 2 * kind + part][shard] = refs[shard][kind, part * SUB : (part + 1) * SUB, :]


def ahead_kernel(place, first, first_got, second, second_got, first_ref, second_ref):
    for own, got, out in ((first, first_got, first_ref), (second, second_got, second_ref)):
        out[0] = own[...]
        out[1] = got[...]


def pack_hidden_kernel(place, *refs):
    for part in range(2):
        for side in range(2):
            for near in range(2):
                for shard in range(3):
                    row = (part * 2 + near) * 288 + shard * PIECE + side * SUB
                    refs[4][row : row + SUB, :] = refs[2 * part + side][near, shard]


def norm1_kernel(place, tokens_ref, gain_ref, shift_ref, h1_ref):
    normed, _ = norm_stats(tokens_ref[...].astype(F32))
    h1_ref[...] = (normed * line(gain_ref) + line(shift_ref)).astype(BF16)


def attend_kernel(shard, place, shift_ref, h1_ref, bias_ref, *refs):
    if shard == 0:
        weight_ref, project_ref, context_ref, lse_ref = refs
    else:
        near_ref, far_ref, weight_ref, project_ref, context_ref, lse_ref = refs
        for slot in range(BLOCK):
            ref = far_ref if slot % 2 else near_ref
            piece = ref[slot // 2] if shard == 1 else ref[shard - 2, slot // 2]
            weight_ref[pl.ds(pl.multiple_of((place[0] ^ slot) * PIECE, 16), PIECE), :] = piece
    h1 = h1_ref[...]
    bias = bias_ref[...]
    for which in range(3):
        rows = slice(which * 192, which * 192 + 192)
        values = nt(weight_ref[rows, :], h1)
        if which != 1:
            first = 16 if which == 0 else 20
            values = values + jnp.concatenate([bias[:, first + i : first + i + 1] for i in range(4)], axis=0)
        if which == 0:
            values = values * HEAD_DIM**-0.5
        project_ref[rows, :] = values.astype(BF16)
    for item in range(h1.shape[0] // SLOTS):
        columns = slice(item * SLOTS, item * SLOTS + SLOTS)
        shift = shift_ref[:, item : item + 1]
        for head in range(HEADS_OWN):
            query, key, value = (
                project_ref[part * 192 + head * 64 : part * 192 + head * 64 + 64, columns] for part in range(3)
            )
            scores = tn(key, query) + shift
            top = jnp.max(scores, axis=0, keepdims=True)
            exps = jnp.exp(scores - top)
            total = jnp.sum(exps, axis=0, keepdims=True)
            probs = (exps * (1.0 / total)).astype(BF16)
            lse_ref[item * HEADS_OWN + head : item * HEADS_OWN + head + 1, :] = top + jnp.log(total)
            context_ref[head * 64 : head * 64 + 64, columns] = nn(value, probs).astype(BF16)


def attend(call, shard, place, shift, h1, bias, weights):
    rows = h1.shape[0]
    outs = (half(576, rows), half(192, rows), flat(HEADS_OWN * rows // SLOTS, SLOTS))
    if shard:
        outs = (half(D, D),) + outs
    got = call(functools.partial(attend_kernel, shard), outs, place, shift, h1, bias, *weights)
    return got if shard else (weights[0], *got)


def middle_kernel(place, tokens_ref, out_bias_ref, gain_ref, shift_ref, *refs):
    contexts, weights, (middle_ref, h2_ref) = refs[:4], refs[4:8], refs[8:]
    total = tokens_ref[...].astype(F32) + line(out_bias_ref)
    context = jnp.concatenate([ref[...] for ref in contexts], axis=0)
    weight = jnp.concatenate([ref[576:768, :] for ref in weights], axis=0)
    total = total + tn(context, weight)
    middle_ref[...] = total
    normed, _ = norm_stats(total)
    h2_ref[...] = (normed * line(gain_ref) + line(shift_ref)).astype(BF16)


def target_of(part, near, side):
    return near + 2 * side if part == 0 else side + 2 * near


def attend_back_kernel(count, place, shift_ref, dmid_ref, h1_ref, project_ref, context_ref, lse_ref, weight_ref, *refs):
    dproject_ref, sums_ref, send_ref, keep_ref, whole = refs[-5:]
    order = count - 1
    if order:
        send_ref[0] = refs[0][0]
        keep_ref[0] = refs[1][0]
    dmid = dmid_ref[...]
    dcontext = nt(weight_ref[576:768, :], dmid).astype(BF16)
    for item in range(dmid.shape[0] // SLOTS):
        columns = slice(item * SLOTS, item * SLOTS + SLOTS)
        shift = shift_ref[:, item : item + 1]
        for head in range(HEADS_OWN):
            query, key, value = (
                project_ref[part * 192 + head * 64 : part * 192 + head * 64 + 64, columns] for part in range(3)
            )
            dctx = dcontext[head * 64 : head * 64 + 64, columns]
            lse = lse_ref[item * HEADS_OWN + head : item * HEADS_OWN + head + 1, :]
            probs = jnp.exp(tn(key, query) + (shift - lse))
            dvalue = nt(dctx, probs.astype(BF16))
            dprobs = tn(value, dctx)
            delta = jnp.sum(probs * dprobs, axis=0, keepdims=True)
            dscores = (probs * (dprobs - delta)).astype(BF16)
            dquery = nn(key, dscores) * HEAD_DIM**-0.5
            dkey = nt(query, dscores)
            for part, grad in enumerate((dquery, dkey, dvalue)):
                dproject_ref[part * 192 + head * 64 : part * 192 + head * 64 + 64, columns] = grad.astype(BF16)
    sums_ref[...] = jnp.zeros(sums_ref.shape, F32)
    for which in (0, 2):
        total = row_sum(dproject_ref[which * 192 : which * 192 + 192, :].astype(F32))
        for i in range(4):
            at = 16 + which * 2 + i
            sums_ref[:, at : at + 1] = total[i * SUB : (i + 1) * SUB, :]
    whole[0:576, :] = nn(dproject_ref[...], h1_ref[...]).astype(BF16)
    whole[576:768, :] = nn(context_ref[...], dmid).astype(BF16)
    for core, part, near, side in PLACES:
        ref = send_ref if core else keep_ref
        ref[order, target_of(part, near, side), part * SUB : (part + 1) * SUB, :] = whole[
            pl.ds(row_of(place[0], core, part, near, side), SUB), :]


def attend_back(call, place, shift, dmid, h1, project, context, lse, weight, before=()):
    rows = h1.shape[0]
    count = 2 if before else 1
    outs = (half(576, rows), flat(SUB, 128), half(count, 4, PIECE, D), half(count, 4, PIECE, D))
    return call(functools.partial(attend_back_kernel, count), outs, place, shift, dmid, h1, project, context, lse,
                weight, *before, scratch=[half(D, D)])


def norm1_back_kernel(place, tokens_ref, dmid_ref, gain_ref, *refs):
    grads, weights, (out_ref, sums_ref) = refs[:4], refs[4:8], refs[8:]
    total = tn(grads[0][...], weights[0][0:576, :])
    for grad_ref, weight_ref in zip(grads[1:], weights[1:]):
        total = total + tn(grad_ref[...], weight_ref[0:576, :])
    normed, factor = norm_stats(tokens_ref[...].astype(F32))
    out_ref[...] = dmid_ref[...] + norm_back(normed, factor, line(gain_ref), total)
    sums_ref[0:1, :] = column_sum(total * normed)
    sums_ref[1:2, :] = column_sum(total)


def bias_columns(bias_refs, groups):
    parts = []
    for group in groups:
        for bias in bias_refs:
            for side in (0, 1):
                parts.append(bias[:, 2 * group + side : 2 * group + side + 1])
    return parts


def up_kernel(groups, place, h2_ref, grad_ref, weight_ref, bias_ref, bias23_ref, act_ref, slope_ref, *outs):
    own = len(groups) == 8
    h2, grad = h2_ref[...], grad_ref[...]
    size = 2 * PIECE if own else 3 * PIECE
    biases = [bias_ref[...]] if own else [bias_ref[...], bias23_ref[0], bias23_ref[1]]
    for index in range(4):
        rows = slice(index * size, (index + 1) * size)
        mine = groups[2 * index : 2 * index + 2] if own else groups[index : index + 1]
        pre = nt(weight_ref[rows, :], h2) + jnp.concatenate(bias_columns(biases, mine), axis=0)
        below = 0.5 * (1.0 + lax.erf(pre * (2.0**-0.5)))
        act = (pre * below).astype(BF16)
        act_ref[rows, :] = act
        slope_ref[rows, :] = (below + pre * (jnp.exp(-0.5 * pre * pre) * ((2.0 * jnp.pi) ** -0.5))).astype(BF16)
        product = nn(act, grad).astype(BF16)
        if own:
            outs[index // 2][2 * (index % 2) : 2 * (index % 2) + 2] = product.reshape(2, PIECE, D)
        else:
            outs[0][index] = product.reshape(3, PIECE, D)


def up_own(call, place, h2, grad, bias, bias23, weight):
    rows = h2.shape[0]
    outs = (half(D, rows), half(D, rows), half(4, PIECE, D), half(4, PIECE, D))
    return call(functools.partial(up_kernel, list(range(8))), outs, place, h2, grad, weight, bias, bias23)


def up_rest(call, far, place, h2, grad, bias1, bias23, weight):
    rows = h2.shape[0]
    outs = (half(1152, rows), half(1152, rows), half(4, 3, PIECE, D))
    groups = list(range(4 * far, 4 * far + 4))
    return call(functools.partial(up_kernel, groups), outs, place, h2, grad, weight, bias1, bias23)


def down_kernel(own, place, h2_ref, grad_ref, slope_ref, weight_ref, dpre_ref, sums_ref, *outs):
    h2, grad = h2_ref[...], grad_ref[...]
    size = 2 * PIECE if own else 3 * PIECE
    sums_ref[...] = jnp.zeros(sums_ref.shape, F32)
    for index in range(4):
        rows = slice(index * size, (index + 1) * size)
        dpre = (nt(weight_ref[rows, :], grad) * slope_ref[rows, :].astype(F32)).astype(BF16)
        dpre_ref[rows, :] = dpre
        total = row_sum(dpre.astype(F32))
        for i in range(size // SUB):
            at = index * (size // SUB) + i
            sums_ref[:, at : at + 1] = total[i * SUB : (i + 1) * SUB, :]
        product = nn(dpre, h2).astype(BF16)
        if own:
            outs[index // 2][2 * (index % 2) : 2 * (index % 2) + 2] = product.reshape(2, PIECE, D)
        else:
            outs[0][index] = product.reshape(3, PIECE, D)


def down_own(call, place, h2, grad, slope, weight):
    rows = h2.shape[0]
    outs = (half(D, rows), flat(SUB, 128), half(4, PIECE, D), half(4, PIECE, D))
    return call(functools.partial(down_kernel, True), outs, place, h2, grad, slope, weight)


def down_rest(call, place, h2, grad, slope, weight):
    rows = h2.shape[0]
    outs = (half(1152, rows), flat(SUB, 128), half(4, 3, PIECE, D))
    return call(functools.partial(down_kernel, False), outs, place, h2, grad, slope, weight)


def norm2_back_kernel(place, middle_ref, grad_ref, gain_ref, *refs):
    grads, weights, (dmid_ref, rounded_ref, sums_ref) = refs[:3], refs[3:6], refs[6:]
    total = tn(grads[0][...], weights[0][...])
    for dpre_ref, weight_ref in zip(grads[1:], weights[1:]):
        total = total + tn(dpre_ref[...], weight_ref[...])
    normed, factor = norm_stats(middle_ref[...])
    grad = grad_ref[...].astype(F32)
    dmid = grad + norm_back(normed, factor, line(gain_ref), total)
    rounded = dmid.astype(BF16)
    dmid_ref[...] = dmid
    rounded_ref[...] = rounded
    sums_ref[0:1, :] = column_sum(rounded.astype(F32))
    sums_ref[1:2, :] = column_sum(total * normed)
    sums_ref[2:3, :] = column_sum(total)
    sums_ref[3:4, :] = column_sum(grad)


def layer_out_kernel(place, middle_ref, bias_ref, *refs):
    acts, weights, (out_ref,) = refs[:3], refs[3:6], refs[6:]
    total = middle_ref[...] + line(bias_ref)
    for act_ref, weight_ref in zip(acts, weights):
        total = total + tn(act_ref[...], weight_ref[...])
    out_ref[...] = total.astype(BF16)


def added(left, right):
    return (left.astype(F32) + right.astype(F32)).astype(BF16)


def core_add_kernel(layout, order, place, *refs):
    count = len(layout)
    keeps, gots, (x_ref, y_ref, stay_ref) = refs[:count], refs[count : 2 * count], refs[2 * count :]
    for source, held in enumerate(layout):
        for group in range(4):
            for at, shard in enumerate(held):
                index = (group,) if len(held) == 1 else (group, at)
                value = added(keeps[source][index], gots[source][index])
                spot = order.index(shard)
                if group % 2 == 0:
                    stay_ref[spot, group // 2] = value
                elif group == 1:
                    x_ref[spot] = value
                else:
                    y_ref[spot] = value


def plane_add_kernel(place, stay_ref, x_ref, y_ref, *outs):
    for spot in range(stay_ref.shape[0]):
        ref = outs[spot // 2]
        ref[spot % 2, 0] = added(stay_ref[spot, 0], x_ref[spot])
        ref[spot % 2, 1] = added(stay_ref[spot, 1], y_ref[spot])


def z_add_kernel(place, keep_ref, got_ref, z_ref, stay_ref):
    stay_ref[...] = added(keep_ref[0], got_ref[0])
    z_ref[...] = added(keep_ref[1], got_ref[1])


def last_z_kernel(place, keep_ref, got_ref, *refs):
    if len(refs) == 1:
        refs[0][...] = added(keep_ref[...], got_ref[...])
    else:
        before_ref, outs = refs[0], refs[1:]
        for part in range(2):
            outs[part][0] = before_ref[part]
            outs[part][1] = added(keep_ref[part], got_ref[part])


def turned_kernel(place, first, first_got, second, second_got, first_ref, second_ref):
    for value, got, out in ((first, first_got, first_ref), (second, second_got, second_ref)):
        out[:, 0:SUB, :] = added(value[:, 0:SUB, :], got[:, SUB:PIECE, :])
        out[:, SUB:PIECE, :] = added(value[:, SUB:PIECE, :], got[:, 0:SUB, :])


def heads_core_kernel(place, odd_ref, odd_got, even_ref, even_got, *outs):
    for keep_ref, got_ref, held in ((odd_ref, odd_got, (1, 3)), (even_ref, even_got, (2, 0))):
        for at, shard in enumerate(held):
            for target in range(4):
                outs[target][shard] = added(keep_ref[at, target], got_ref[at, target])


def sum_of(refs, index):
    total = refs[0][index].astype(F32)
    for ref in refs[1:]:
        total = total + ref[index].astype(F32)
    return total.astype(BF16)


def heads_plane_kernel(place, *refs):
    for shard in range(4):
        refs[4 + shard][...] = sum_of(refs[:4], shard)


def heads_z_kernel(place, *refs):
    refs[4][...] = sum_of(refs[:4], Ellipsis)


def finish_kernel(kind, which, place, near_ref, far_ref, *refs):
    whole = refs[0] if kind == "rows" else refs[-1]
    for core, part, near, side in PLACES:
        ref = far_ref if core else near_ref
        if kind == "heads":
            block = ref[target_of(part, near, side), part * SUB : (part + 1) * SUB, :]
        else:
            block = ref[part * 2 + near, which, side * SUB : (side + 1) * SUB, :]
        whole[pl.ds(row_of(place[0], core, part, near, side), SUB), :] = block.astype(whole.dtype)
    if kind == "columns":
        refs[0][...] = whole[...].T.astype(F32)
    if kind == "heads":
        for index in range(4):
            refs[index][...] = whole[index * 192 : index * 192 + 192, :].astype(F32)


def small_pack_kernel(place, in_ref, mid_ref, own_ref, near_ref, far_ref, head0, head1, head2, head3, out_ref,
                      column_ref):
    column_ref[...] = jnp.zeros(column_ref.shape, F32)
    for shard in range(4):
        for index, spot in enumerate(PLACES):
            if shard == 0:
                ref, at = own_ref, index
            else:
                ref, at = (far_ref if spot[0] else near_ref), (index % 8) // 2 * 6 + (shard - 1) * 2 + spot[3]
            column_ref[pl.ds(row_of(place[0], *spot), SUB), shard : shard + 1] = ref[:, at : at + 1]
    for shard, ref in enumerate((head0, head1, head2, head3)):
        for index in range(8):
            low = index // 4 * 256 + index % 4 * SUB
            column_ref[low : low + SUB, 4 + shard : 5 + shard] = ref[:, 16 + index : 17 + index]
    out_ref[0:2, :] = in_ref[...]
    out_ref[2:6, :] = mid_ref[...]
    out_ref[6:14, :] = column_ref[...].T[0:8, :]
    out_ref[14:16, :] = jnp.zeros((2, D), F32)


def small_sum(turn, value_ref, got_ref, out_ref):
    out_ref[0:6, :] = value_ref[0:6, :] + got_ref[0:6, :]
    for shard in range(4):
        for first in (6, 10):
            mine, other = first + shard, first + (shard ^ turn)
            out_ref[mine : mine + 1, :] = value_ref[mine : mine + 1, :] + got_ref[other : other + 1, :]


def small_add_kernel(turn, place, value_ref, got_ref, out_ref):
    small_sum(turn, value_ref, got_ref, out_ref)


def small_last_kernel(place, value_ref, got_ref, *refs):
    total = refs[-1]
    small_sum(2, value_ref, got_ref, total)
    for index in range(7):
        refs[index][...] = total[index : index + 1, :].reshape(D)
    refs[7][...] = total[10:11, 0:192].reshape(192)
    refs[8][...] = total[10:11, 256:448].reshape(192)


def shards(dp_size, z_size, tokens, cotangent, patch_count, word_mask, norm1_gain, norm1_shift, query_weight,
           query_bias, key_weight, value_weight, value_bias, out_weight, out_bias, norm2_gain, norm2_shift,
           up_weight, up_bias, down_weight, down_bias):
    rows = tokens.shape[0]
    place = jnp.stack([lax.axis_index("dp") % BLOCK, lax.axis_index("tensor")]).astype(jnp.int32)
    groups = [list(range(i, dp_size, BLOCK)) for i in range(BLOCK)]
    call = Chain()

    def swap(value, bit):
        return lax.ppermute(call.tie(value), "dp", [(i, i ^ bit) for i in range(dp_size)])

    def swap_z(value, bit):
        return lax.ppermute(call.tie(value), "tensor", [(i, i ^ bit) for i in range(z_size)])

    heads_own, heads_piece = call(heads_prep_kernel, (half(D, D), half(PIECE, D)), place, query_weight.T,
                                  key_weight.T, value_weight.T, out_weight)
    heads_at = [swap_z(heads_piece, bit) for bit in (1, 2, 3)]
    bias, shift = call(
        small_prep_kernel, (flat(SUB, 128), flat(SLOTS, 8)), place, patch_count, word_mask, up_bias, query_bias,
        value_bias, scratch=[flat(D + 384, 8), flat(8, SLOTS)], scalars=2)
    h1 = call(norm1_kernel, half(rows, D), place, tokens, norm1_gain, norm1_shift)
    parts = [attend(call, 0, place, shift, h1, bias, [heads_own])]
    up_order, piece = call(functools.partial(hidden_prep_kernel, 0), (half(D, D), half(2, PIECE, D)), place, up_weight,
                           scratch=[half(D, D)])
    down_order, piece = call(functools.partial(hidden_prep_kernel, 1), (half(D, D), half(2, PIECE, D)), place,
                             down_weight, piece)

    near1 = [heads_at[0]] + [swap(heads_at[0], bit) for bit in (2, 4, 6)]
    bias1 = swap_z(bias, 1)
    heads23 = call(pack_kernel, half(2, PIECE, D), place, *heads_at[1:])
    near23 = [heads23] + [swap(heads23, bit) for bit in (2, 4, 6)]
    bias_pair = call(pack_kernel, flat(2, SUB, 128), place, bias, bias1)
    pack1 = call(pack_kernel, half(4, PIECE, D), place, *near1)
    far1 = swap(pack1, 1)
    pieces = [swap_z(piece, bit) for bit in (1, 2)]
    parts.append(attend(call, 1, place, shift, h1, bias1, [pack1, far1]))
    bias23 = swap_z(bias_pair, 2)
    pieces.append(swap_z(pieces[1], 1))
    near23[0] = lax.optimization_barrier((near23[0], bias23, *pieces[:2]))[0]
    pack23 = call(pack_heads_kernel, half(2, 4, PIECE, D), place, *near23)
    far23 = swap(pack23, 1)
    halves = call(split_kernel, (half(3, SUB, D),) * 4, place, *pieces)
    halves = list(zip(halves, [swap(value, bit) for value, bit in zip(halves, (2, 4, 2, 4))]))
    parts.append(attend(call, 2, place, shift, h1, bias23[0], [pack23, far23]))

    def ahead(first, second):
        first, second = call(ahead_kernel, (half(2, 3, SUB, D),) * 2, place, *first, *second)
        return first, swap(first, 4), second, swap(second, 2)

    up_near = ahead(*halves[:2])
    parts.append(attend(call, 3, place, shift, h1, bias23[1], [pack23, far23]))
    down_near = ahead(*halves[2:])
    weight, project, context, lse = zip(*parts)
    middle, h2 = call(middle_kernel, (flat(rows, D), half(rows, D)), place, tokens, out_bias, norm2_gain, norm2_shift,
                      *context, *weight)
    act0, slope0, keep0, send0 = up_own(call, place, h2, cotangent, bias, bias23, up_order)
    up_near_w = call(pack_hidden_kernel, half(1152, D), place, *up_near)
    up_far_w = swap(up_near_w, 1)
    act1, slope1, keep1 = up_rest(call, False, place, h2, cotangent, bias1, bias23, up_near_w)
    act2, slope2, send1 = up_rest(call, True, place, h2, cotangent, bias1, bias23, up_far_w)

    mlp = ((0,), (1, 2, 3))
    order = (0, 2, 1, 3)

    def core_sums(keeps, gots):
        to_x, to_y, stay = call(
            functools.partial(core_add_kernel, mlp, order),
            (half(4, PIECE, D), half(4, PIECE, D), half(4, 2, PIECE, D)), place, *keeps, *gots)
        return stay, swap(to_x, 2), swap(to_y, 4)

    def plane_sums(state):
        return call(plane_add_kernel, (half(2, 2, PIECE, D), half(2, 2, PIECE, D)), place, *state)

    def z_sums(stay, got):
        return call(z_add_kernel, (half(2, PIECE, D), half(2, PIECE, D)), place, stay, got)

    dpre0, sums0, up_keep0, up_send0 = down_own(call, place, h2, cotangent, slope0, down_order)
    down_near_w = call(pack_hidden_kernel, half(1152, D), place, *down_near)
    down_far_w = swap(down_near_w, 1)
    got0, got1 = swap(send0, 1), swap(send1, 1)
    dpre1, sums1, up_keep1 = down_rest(call, place, h2, cotangent, slope1, down_near_w)
    down_sum = core_sums([keep0, keep1], [got0, got1])
    dpre2, sums2, up_send1 = down_rest(call, place, h2, cotangent, slope2, down_far_w)
    dmid, dmid_b, mid_sums = call(
        norm2_back_kernel, (flat(rows, D), half(rows, D), flat(4, D)), place, middle, cotangent, norm2_gain,
        dpre0, dpre1, dpre2, up_order, up_near_w, up_far_w)
    def attention_back(t, before=()):
        return attend_back(call, place, shift, dmid_b, h1, project[t], context[t], lse[t], weight[t], before)

    back1 = attention_back(1)
    stay, go = plane_sums(down_sum)
    down_z = stay, swap_z(go, 1)
    up_gots = [swap(up_send0, 1), swap(up_send1, 1)]
    back3 = attention_back(3, back1[2:])
    up_sum = core_sums([up_keep0, up_keep1], up_gots)
    odd_got = swap(back3[2], 1)
    back2 = attention_back(2)
    back0 = attention_back(0, back2[2:])
    go, stay = z_sums(*down_z)
    down_z = stay, swap_z(go, 2)
    dproject, head_sums = zip(*[value[:2] for value in (back0, back1, back2, back3)])
    input_grad, in_sums = call(norm1_back_kernel, (flat(rows, D), flat(2, D)), place, tokens, dmid, norm1_gain,
                               *dproject, *weight)
    stay, go = plane_sums(up_sum)
    down_last = call(last_z_kernel, half(2, PIECE, D), place, *down_z)
    even_got = swap(back0[2], 1)
    up_z = stay, swap_z(go, 1)
    small = call(small_pack_kernel, flat(16, D), place, in_sums, mid_sums, sums0, sums1, sums2, *head_sums,
                 scratch=[flat(D, 8)])
    heads_own_sum, to_x, to_y, to_xy = call(heads_core_kernel, (half(4, PIECE, D),) * 4, place, back3[3], odd_got,
                                            back0[3], even_got)
    heads_plane = [heads_own_sum, swap(to_x, 2), swap(to_y, 4), swap(to_xy, 6)]
    layer_out = call(layer_out_kernel, half(rows, D), place, middle, down_bias, act0, act1, act2, down_order,
                     down_near_w, down_far_w)
    go, stay = z_sums(*up_z)
    up_z = stay, swap_z(go, 2)

    def small_sums(turn, value, got):
        return call(functools.partial(small_add_kernel, turn), flat(16, D), place, value, got)

    small = small_sums(0, small, swap(small, 1))
    parts = call(heads_plane_kernel, (half(PIECE, D),) * 4, place, *heads_plane)
    heads_z = [parts[0]] + [swap_z(parts[bit], bit) for bit in (1, 2, 3)]
    small = small_sums(0, small, swap(small, 2))
    first, second = call(last_z_kernel, (half(2, PIECE, D),) * 2, place, *up_z, down_last)
    first_got, second_got = swap(first, 4), swap(second, 2)
    mine = call(heads_z_kernel, half(PIECE, D), place, *heads_z)
    if dp_size > BLOCK:
        mine = lax.psum(mine, "dp", axis_index_groups=groups)
    heads_near = [mine] + [swap(mine, bit) for bit in (2, 4, 6)]
    first, second = call(turned_kernel, (half(2, PIECE, D),) * 2, place, first, first_got, second, second_got)
    if dp_size > BLOCK:
        first, second = lax.psum((first, second), "dp", axis_index_groups=groups)
    mlp_near = [first, swap(first, 2), second, swap(second, 4)]
    small_got = swap(small, 4)
    mlp_near = call(pack_kernel, half(4, 2, PIECE, D), place, *mlp_near)
    mlp_far = swap(mlp_near, 1)
    small = small_sums(0, small, small_got)
    if dp_size > BLOCK:
        small = lax.psum(small, "dp", axis_index_groups=groups)
    small_got = swap_z(small, 1)
    down_weight_grad = call(functools.partial(finish_kernel, "rows", 0), flat(D, D), place, mlp_near, mlp_far)
    heads_near = call(pack_kernel, half(4, PIECE, D), place, *heads_near)
    heads_far = swap(heads_near, 1)
    small = small_sums(1, small, small_got)
    small_got = swap_z(small, 2)
    up_weight_grad = call(functools.partial(finish_kernel, "columns", 1), flat(D, D), place, mlp_near, mlp_far,
                          scratch=[half(D, D)])
    query_grad, key_grad, value_grad, out_weight_grad = call(
        functools.partial(finish_kernel, "heads", 0), (flat(192, D),) * 4, place, heads_near, heads_far,
        scratch=[half(D, D)])
    vectors = call(small_last_kernel, (flat(D),) * 7 + (flat(192),) * 2, place, small, small_got,
                   scratch=[flat(16, D)])
    return (
        layer_out, input_grad, vectors[0], vectors[1], query_grad.T, vectors[7], key_grad.T, value_grad.T, vectors[8],
        out_weight_grad, vectors[2], vectors[3], vectors[4], up_weight_grad, vectors[6], down_weight_grad, vectors[5],
    )


def solution(mesh):
    rows = P(("dp", "tensor"), None)
    columns = P(None, "tensor")
    part = P("tensor")
    part_rows = P("tensor", None)
    whole = P()
    return jax.shard_map(
        functools.partial(shards, mesh.shape["dp"], mesh.shape["tensor"]),
        mesh=mesh,
        in_specs=(rows, rows, P("dp"), P("dp", None), whole, whole, columns, part, columns, columns, part,
                  part_rows, whole, whole, whole, columns, part, part_rows, whole),
        out_specs=(rows, rows, whole, whole, columns, part, columns, columns, part, part_rows, whole, whole,
                   whole, columns, part, part_rows, whole),
        check_vma=False,
    )
```

```python
import functools
import math

import jax
import jax.numpy as jnp
from jax import lax
from jax.experimental import pallas as pl
from jax.experimental.pallas import tpu as pltpu
from jax.sharding import PartitionSpec as P

D = 768
HEAD_DIM = 64
HEADS_OWN = 3
ITEMS_OWN = 2
WORDS = 40
SLOTS = 256
NORM_EPS = 1e-05
MASKED = -1e30
BLOCK = 8
PIECE = D // BLOCK
SUB = PIECE // 2
F32 = jnp.float32
BF16 = jnp.bfloat16
STACK = 6 * 1024 * 1024


def nn(left, right):
    return lax.dot_general(left, right, (((1,), (0,)), ((), ())), preferred_element_type=F32)


def nt(left, right):
    return lax.dot_general(left, right, (((1,), (1,)), ((), ())), preferred_element_type=F32)


def tn(left, right):
    return lax.dot_general(left, right, (((0,), (0,)), ((), ())), preferred_element_type=F32)


def norm_stats(values):
    mean = jnp.mean(values, axis=-1, keepdims=True)
    centered = values - mean
    factor = lax.rsqrt(jnp.mean(centered * centered, axis=-1, keepdims=True) + NORM_EPS)
    return centered * factor, factor


def norm_back(normed, factor, gain, grad):
    scaled = grad * gain
    mean_scaled = jnp.mean(scaled, axis=-1, keepdims=True)
    mean_product = jnp.mean(scaled * normed, axis=-1, keepdims=True)
    return factor * (scaled - mean_scaled - normed * mean_product)


def column_sum(values):
    return jnp.sum(values, axis=0, keepdims=True)


def row_sum(values):
    return jnp.sum(values, axis=1, keepdims=True)


def flat(*size):
    return jax.ShapeDtypeStruct(size, F32)


def half(*size):
    return jax.ShapeDtypeStruct(size, BF16)


def size_of(shape, dtype):
    shape = (1,) * (2 - len(shape)) + tuple(shape)
    return math.prod(shape[:-2]) * -(-shape[-2] // 8) * 8 * -(-shape[-1] // 128) * 128 * jnp.dtype(dtype).itemsize


class Chain:
    def __init__(self):
        self.last = None

    def tie(self, value):
        return value if self.last is None else lax.optimization_barrier((value, self.last))[0]

    def __call__(self, body, outs, *args, scratch=(), scalars=1):
        args = args[:scalars] + (self.tie(args[scalars]),) + args[scalars + 1 :]
        got = kernel(body, outs, *args, scratch=scratch, scalars=scalars)
        self.last = jax.tree.leaves(got)[-1]
        return got


def kernel(body, outs, *args, scratch=(), scalars=1):
    held = list(args[scalars:]) + jax.tree.leaves(outs) + list(scratch)
    limit = STACK + sum(size_of(h.shape, h.dtype) for h in held)
    return pl.pallas_call(
        body,
        name=(body.func if isinstance(body, functools.partial) else body).__name__,
        out_shape=outs,
        in_specs=[pl.BlockSpec(memory_space=pltpu.SMEM)] * scalars
        + [pl.BlockSpec(memory_space=pltpu.VMEM)] * (len(args) - scalars),
        out_specs=jax.tree.map(lambda _: pl.BlockSpec(memory_space=pltpu.VMEM), outs),
        scratch_shapes=[pltpu.VMEM(s.shape, s.dtype) for s in scratch],
        compiler_params=pltpu.CompilerParams(vmem_limit_bytes=limit),
        cost_estimate=pl.CostEstimate(flops=1, bytes_accessed=1, transcendentals=1),
    )(*args)


def line(ref):
    return ref[...].reshape(1, -1)


def row_of(me, core, part, near, side):
    mine, x, y = me & 1, (me >> 1) & 1, me >> 2
    ahead, beside = (x, y) if part == 0 else (y, x)
    row = part * (D // 2) + ((ahead ^ near) * 2 + (mine ^ core)) * PIECE + (beside ^ side) * SUB
    return pl.multiple_of(row, 16)


PLACES = [(core, part, near, side) for core in (0, 1) for part in (0, 1) for near in (0, 1) for side in (0, 1)]


def heads_prep_kernel(place, query_ref, key_ref, value_ref, out_ref, whole_ref):
    for index, ref in enumerate((query_ref, key_ref, value_ref, out_ref)):
        whole_ref[index * 192 : index * 192 + 192, :] = ref[...]


def hidden_prep_kernel(which, place, weight_ref, *refs):
    if which == 0:
        order_ref, piece_ref, scratch = refs
        scratch[...] = weight_ref[...].T
        weight_ref = scratch
    else:
        before_ref, order_ref, piece_ref = refs
        piece_ref[0] = before_ref[0]
    for index, (core, part, near, side) in enumerate(PLACES):
        block = weight_ref[pl.ds(row_of(place[0], core, part, near, side), SUB), :]
        order_ref[index * SUB : (index + 1) * SUB, :] = block
        if core + near + side == 0:
            piece_ref[which, part * SUB : (part + 1) * SUB, :] = block


def small_prep_kernel(place, keys_ref, vectors_ref, bias_ref, shift_ref, column_ref, rows_ref):
    bias_ref[...] = jnp.zeros(bias_ref.shape, F32)
    size = vectors_ref.shape[0]
    column_ref[...] = jnp.broadcast_to(line(vectors_ref), (8, size)).T
    for index, spot in enumerate(PLACES):
        bias_ref[:, index : index + 1] = column_ref[pl.ds(row_of(place[0], *spot), SUB), 0:1]
    for index in range(8):
        low = D + index * SUB
        bias_ref[:, 16 + index : 17 + index] = column_ref[low : low + SUB, 0:1]
    lane = lax.broadcasted_iota(jnp.int32, (1, SLOTS), 1)
    rows_ref[...] = jnp.zeros(rows_ref.shape, F32)
    for item in range(ITEMS_OWN):
        row = keys_ref[pl.ds(place[1] * ITEMS_OWN + item, 1), :]
        count = row[:, WORDS : WORDS + 1]
        rows_ref[item : item + 1, 0:WORDS] = row[:, 0:WORDS].astype(F32)
        live = jnp.where(lane < WORDS, rows_ref[item : item + 1, :], jnp.where(lane - WORDS < count, 1.0, 0.0))
        rows_ref[item : item + 1, :] = jnp.where(live > 0, 0.0, MASKED)
    shift_ref[...] = rows_ref[...].T


def join_kernel(place, *refs):
    low = 0
    for ref in refs[:-1]:
        refs[-1][low : low + ref.shape[0], :] = ref[...]
        low += ref.shape[0]


def pack_kernel(place, *refs):
    for index, ref in enumerate(refs[:-1]):
        refs[-1][index] = ref[...]


def pack_heads_kernel(place, *refs):
    for index, ref in enumerate(refs[:-1]):
        refs[-1][:, index] = ref[...]


def split_kernel(place, *refs):
    for shard in range(3):
        for kind in range(2):
            for part in range(2):
                refs[3 + 2 * kind + part][shard] = refs[shard][kind, part * SUB : (part + 1) * SUB, :]


def ahead_kernel(place, first, first_got, second, second_got, first_ref, second_ref):
    for own, got, out in ((first, first_got, first_ref), (second, second_got, second_ref)):
        out[0] = own[...]
        out[1] = got[...]


def pack_hidden_kernel(place, *refs):
    for part in range(2):
        for side in range(2):
            for near in range(2):
                for shard in range(3):
                    row = (part * 2 + near) * 288 + shard * PIECE + side * SUB
                    refs[4][row : row + SUB, :] = refs[2 * part + side][near, shard]


def norm1_kernel(place, tokens_ref, gain_ref, shift_ref, h1_ref):
    normed, _ = norm_stats(tokens_ref[...].astype(F32))
    h1_ref[...] = (normed * line(gain_ref) + line(shift_ref)).astype(BF16)


def attend_kernel(shard, place, shift_ref, h1_ref, bias_ref, *refs):
    if shard == 0:
        weight_ref, project_ref, context_ref, lse_ref = refs
    else:
        near_ref, far_ref, weight_ref, project_ref, context_ref, lse_ref = refs
        for slot in range(BLOCK):
            ref = far_ref if slot % 2 else near_ref
            weight_ref[pl.ds(pl.multiple_of((place[0] ^ slot) * PIECE, 16), PIECE), :] = ref[shard - 1, slot // 2]
    h1 = h1_ref[...]
    bias = bias_ref[...]
    zero = jnp.zeros((192, 1), F32)
    columns = [jnp.concatenate([bias[:, at : at + 1] for at in range(first, first + 4)], axis=0) for first in (16, 20)]
    values = nt(weight_ref[0:576, :], h1) + jnp.concatenate([columns[0], zero, columns[1]], axis=0)
    project_ref[0:192, :] = (values[0:192] * HEAD_DIM**-0.5).astype(BF16)
    project_ref[192:576, :] = values[192:576].astype(BF16)
    for item in range(h1.shape[0] // SLOTS):
        columns = slice(item * SLOTS, item * SLOTS + SLOTS)
        shift = shift_ref[:, item : item + 1]
        for head in range(HEADS_OWN):
            query, key, value = (
                project_ref[part * 192 + head * 64 : part * 192 + head * 64 + 64, columns] for part in range(3)
            )
            scores = tn(key, query) + shift
            top = jnp.max(scores, axis=0, keepdims=True)
            exps = jnp.exp(scores - top)
            total = jnp.sum(exps, axis=0, keepdims=True)
            probs = (exps * (1.0 / total)).astype(BF16)
            lse_ref[item * HEADS_OWN + head : item * HEADS_OWN + head + 1, :] = top + jnp.log(total)
            context_ref[head * 64 : head * 64 + 64, columns] = nn(value, probs).astype(BF16)


def attend(call, shard, place, shift, h1, bias, weights):
    rows = h1.shape[0]
    outs = (half(576, rows), half(192, rows), flat(HEADS_OWN * rows // SLOTS, SLOTS))
    if shard:
        outs = (half(D, D),) + outs
    got = call(functools.partial(attend_kernel, shard), outs, place, shift, h1, bias, *weights)
    return got if shard else (weights[0], *got)


def middle_kernel(place, tokens_ref, out_bias_ref, gain_ref, shift_ref, *refs):
    contexts, weights, (middle_ref, h2_ref, first_ref, second_ref) = refs[:4], refs[4:8], refs[8:]
    total = tokens_ref[...].astype(F32) + line(out_bias_ref)
    context = jnp.concatenate([ref[...] for ref in contexts], axis=0)
    weight = jnp.concatenate([ref[576:768, :] for ref in weights], axis=0)
    total = total + tn(context, weight)
    middle_ref[...] = total
    normed, _ = norm_stats(total)
    h2 = (normed * line(gain_ref) + line(shift_ref)).astype(BF16)
    h2_ref[...] = h2
    first_ref[...] = h2[: h2.shape[0] // 2]
    second_ref[...] = h2[h2.shape[0] // 2 :]


def target_of(part, near, side):
    return near + 2 * side if part == 0 else side + 2 * near


def attend_back_kernel(place, shift_ref, dmid_ref, h1_ref, project_ref, context_ref, lse_ref, weight_ref, *refs):
    dproject_ref, sums_ref, send_ref, keep_ref, whole = refs
    dmid = dmid_ref[...]
    dcontext = nt(weight_ref[576:768, :], dmid).astype(BF16)
    for item in range(dmid.shape[0] // SLOTS):
        columns = slice(item * SLOTS, item * SLOTS + SLOTS)
        shift = shift_ref[:, item : item + 1]
        for head in range(HEADS_OWN):
            query, key, value = (
                project_ref[part * 192 + head * 64 : part * 192 + head * 64 + 64, columns] for part in range(3)
            )
            dctx = dcontext[head * 64 : head * 64 + 64, columns]
            lse = lse_ref[item * HEADS_OWN + head : item * HEADS_OWN + head + 1, :]
            probs = jnp.exp(tn(key, query) + (shift - lse))
            dvalue = nt(dctx, probs.astype(BF16))
            dprobs = tn(value, dctx)
            delta = jnp.sum(probs * dprobs, axis=0, keepdims=True)
            dscores = (probs * (dprobs - delta)).astype(BF16)
            dquery = nn(key, dscores) * HEAD_DIM**-0.5
            dkey = nt(query, dscores)
            for part, grad in enumerate((dquery, dkey, dvalue)):
                dproject_ref[part * 192 + head * 64 : part * 192 + head * 64 + 64, columns] = grad.astype(BF16)
    sums_ref[...] = jnp.zeros(sums_ref.shape, F32)
    for which in (0, 2):
        total = row_sum(dproject_ref[which * 192 : which * 192 + 192, :].astype(F32))
        for i in range(4):
            at = 16 + which * 2 + i
            sums_ref[:, at : at + 1] = total[i * SUB : (i + 1) * SUB, :]
    whole[0:576, :] = nn(dproject_ref[...], h1_ref[...]).astype(BF16)
    whole[576:768, :] = nn(context_ref[...], dmid).astype(BF16)
    for core, part, near, side in PLACES:
        ref = send_ref if core else keep_ref
        ref[target_of(part, near, side), part * SUB : (part + 1) * SUB, :] = whole[
            pl.ds(row_of(place[0], core, part, near, side), SUB), :]


def attend_back(call, place, shift, dmid, h1, project, context, lse, weight):
    rows = h1.shape[0]
    outs = (half(576, rows), flat(SUB, 128), half(4, PIECE, D), half(4, PIECE, D))
    return call(attend_back_kernel, outs, place, shift, dmid, h1, project, context, lse, weight, scratch=[half(D, D)])


def norm1_back_kernel(place, tokens_ref, dmid_ref, gain_ref, *refs):
    grads, weights, (out_ref, sums_ref) = refs[:4], refs[4:8], refs[8:]
    total = tn(grads[0][...], weights[0][0:576, :])
    for grad_ref, weight_ref in zip(grads[1:], weights[1:]):
        total = total + tn(grad_ref[...], weight_ref[0:576, :])
    normed, factor = norm_stats(tokens_ref[...].astype(F32))
    out_ref[...] = dmid_ref[...] + norm_back(normed, factor, line(gain_ref), total)
    sums_ref[0:1, :] = column_sum(total * normed)
    sums_ref[1:2, :] = column_sum(total)


def bias_columns(biases, groups):
    return jnp.concatenate(
        [bias[:, 2 * group + side : 2 * group + side + 1] for group in groups for bias in biases for side in (0, 1)],
        axis=0)


def blocks(own):
    return [(0, 1, 2, 3)] if own else [(0,), (1,), (2,), (3,)]


def deliver(group, shards, product, x_ref, y_ref, stay_ref):
    for at, shard in enumerate(shards):
        spot = ORDER.index(shard)
        if group % 2 == 0:
            stay_ref[spot, group // 2] = product[at]
        else:
            (x_ref if group == 1 else y_ref)[spot] = product[at]


def deliver_before(before, x_ref, y_ref, stay_ref):
    x_ref[0], y_ref[0], stay_ref[0] = before[0][0], before[1][0], before[2][0]


def up_kernel(own, place, h2_ref, grad_ref, weight_ref, bias_ref, bias23_ref, *refs):
    h2 = h2_ref[...]
    if own:
        act_ref, slope_ref, x_ref, y_ref, stay_ref = refs
        biases, shards = [bias_ref[...]], (0,)
    else:
        before, (act_ref, slope_ref, x_ref, y_ref, stay_ref) = refs[:3], refs[3:]
        deliver_before(before, x_ref, y_ref, stay_ref)
        biases, shards = [bias_ref[...], bias23_ref[0], bias23_ref[1]], (1, 2, 3)
    size = len(shards) * PIECE
    for block in blocks(own):
        rows = slice(block[0] * size, (block[-1] + 1) * size)
        pre = nt(weight_ref[rows, :], h2) + bias_columns(biases, block)
        below = 0.5 * (1.0 + lax.erf(pre * (2.0**-0.5)))
        act = (pre * below).astype(BF16)
        act_ref[rows, :] = act
        slope_ref[rows, :] = (below + pre * (jnp.exp(-0.5 * pre * pre) * ((2.0 * jnp.pi) ** -0.5))).astype(BF16)
        product = nn(act, grad_ref[...]).astype(BF16).reshape(len(block), len(shards), PIECE, D)
        for at, group in enumerate(block):
            deliver(group, shards, product[at], x_ref, y_ref, stay_ref)


def down_kernel(own, place, h2_ref, grad_ref, slope_ref, weight_ref, *refs):
    if own:
        dpre_ref, sums_ref, x_ref, y_ref, stay_ref = refs
        shards = (0,)
    else:
        before, (dpre_ref, sums_ref, x_ref, y_ref, stay_ref) = refs[:3], refs[3:]
        deliver_before(before, x_ref, y_ref, stay_ref)
        shards = (1, 2, 3)
    size = len(shards) * PIECE
    sums_ref[...] = jnp.zeros(sums_ref.shape, F32)
    for block in blocks(own):
        rows = slice(block[0] * size, (block[-1] + 1) * size)
        dpre = (nt(weight_ref[rows, :], grad_ref[...]) * slope_ref[rows, :].astype(F32)).astype(BF16)
        dpre_ref[rows, :] = dpre
        total = row_sum(dpre.astype(F32))
        for i in range(len(block) * size // SUB):
            at = block[0] * (size // SUB) + i
            sums_ref[:, at : at + 1] = total[i * SUB : (i + 1) * SUB, :]
        product = nn(dpre, h2_ref[...]).astype(BF16).reshape(len(block), len(shards), PIECE, D)
        for at, group in enumerate(block):
            deliver(group, shards, product[at], x_ref, y_ref, stay_ref)


def sends(count):
    return half(count, PIECE, D), half(count, PIECE, D), half(count, 2, PIECE, D)


def partner_kernel(parts, place, own_ref, near_ref, own_weight_ref, near_weight_ref, *outs):
    rows = own_ref.shape[1] // 2
    total = tn(own_ref[:, rows:], own_weight_ref[0 : D // 2, :]) + tn(near_ref[:, rows:], near_weight_ref[...])
    size = rows // len(outs)
    for index, ref in enumerate(outs):
        ref[...] = total[index * size : (index + 1) * size].astype(BF16)


def own_rows(own_ref, near_ref, own_weight_ref, near_weight_ref, gots):
    rows = own_ref.shape[1] // 2
    total = tn(own_ref[:, :rows], own_weight_ref[0 : D // 2, :]) + tn(near_ref[:, :rows], near_weight_ref[...])
    return total + jnp.concatenate([ref[...] for ref in gots], axis=0).astype(F32)


def norm2_back_kernel(place, middle_ref, grad_ref, gain_ref, own_ref, near_ref, own_weight_ref, near_weight_ref,
                      first_ref, second_ref, dmid_ref, rounded_ref, sums_ref):
    total = own_rows(own_ref, near_ref, own_weight_ref, near_weight_ref, (first_ref, second_ref))
    normed, factor = norm_stats(middle_ref[...])
    grad = grad_ref[...].astype(F32)
    dmid = grad + norm_back(normed, factor, line(gain_ref), total)
    rounded = dmid.astype(BF16)
    dmid_ref[...] = dmid
    rounded_ref[...] = rounded
    sums_ref[0:1, :] = column_sum(rounded.astype(F32))
    sums_ref[1:2, :] = column_sum(total * normed)
    sums_ref[2:3, :] = column_sum(total)
    sums_ref[3:4, :] = column_sum(grad)


def layer_out_kernel(place, middle_ref, bias_ref, own_ref, near_ref, own_weight_ref, near_weight_ref, got_ref, out_ref):
    total = own_rows(own_ref, near_ref, own_weight_ref, near_weight_ref, (got_ref,))
    out_ref[...] = (total + middle_ref[...] + line(bias_ref)).astype(BF16)


ORDER = (0, 2, 1, 3)


def added(left, right):
    return (left.astype(F32) + right.astype(F32)).astype(BF16)


def plane_add_kernel(place, stay_ref, x_ref, y_ref, *outs):
    for spot in range(stay_ref.shape[0]):
        ref = outs[spot // 2]
        ref[spot % 2, 0] = added(stay_ref[spot, 0], x_ref[spot])
        ref[spot % 2, 1] = added(stay_ref[spot, 1], y_ref[spot])


def z_add_kernel(place, keep_ref, got_ref, z_ref, stay_ref):
    stay_ref[...] = added(keep_ref[0], got_ref[0])
    z_ref[...] = added(keep_ref[1], got_ref[1])


def last_z_kernel(place, keep_ref, got_ref, *refs):
    if len(refs) == 1:
        refs[0][...] = added(keep_ref[...], got_ref[...])
    else:
        before_ref, outs = refs[0], refs[1:]
        for part in range(2):
            outs[part][0] = before_ref[part]
            outs[part][1] = added(keep_ref[part], got_ref[part])


def turned_kernel(place, first, first_got, second, second_got, first_ref, second_ref):
    for value, got, out in ((first, first_got, first_ref), (second, second_got, second_ref)):
        out[:, 0:SUB, :] = added(value[:, 0:SUB, :], got[:, SUB:PIECE, :])
        out[:, SUB:PIECE, :] = added(value[:, SUB:PIECE, :], got[:, 0:SUB, :])


def heads_core_kernel(held, place, *refs):
    outs = refs[-4:]
    for at, shard in enumerate(held):
        for target in range(4):
            outs[target][shard] = added(refs[at][target], refs[2 + at][target])
    for target, ref in enumerate(refs[4:-4]):
        outs[target][1] = ref[0]
        outs[target][3] = ref[1]


def sum_of(refs, index):
    total = refs[0][index].astype(F32)
    for ref in refs[1:]:
        total = total + ref[index].astype(F32)
    return total.astype(BF16)


def two_parts(rows):
    high = rows.astype(BF16).astype(F32)
    return jnp.concatenate([high, rows - high], axis=0).astype(BF16)


def one_part(ref, low):
    rows = ref[low : low + 16, :].astype(F32)
    return rows[0:8] + rows[8:16]


def heads_plane_kernel(place, own_ref, x_ref, y_ref, xy_ref, small_ref, *outs):
    small = small_ref[...]
    for shard in range(4):
        outs[shard][0:PIECE, :] = sum_of((own_ref, x_ref, y_ref, xy_ref), shard)
        rows = [small[0:6], small[6 + shard : 7 + shard], small[10 + shard : 11 + shard]]
        outs[shard][PIECE : PIECE + 16, :] = two_parts(jnp.concatenate(rows, axis=0))


def heads_z_kernel(place, *refs):
    out_ref = refs[4]
    out_ref[0:PIECE, :] = sum_of([ref.at[0:PIECE] for ref in refs[:4]], Ellipsis)
    total = one_part(refs[0], PIECE)
    for ref in refs[1:4]:
        total = total + one_part(ref, PIECE)
    out_ref[PIECE : PIECE + 16, :] = two_parts(total)


def heads_pack_kernel(place, *refs):
    out_ref = refs[4]
    total = one_part(refs[0], PIECE)
    for ref in refs[1:4]:
        total = total + one_part(ref, PIECE)
    for index, ref in enumerate(refs[:4]):
        out_ref[index * PIECE : (index + 1) * PIECE, :] = ref[0:PIECE, :]
    out_ref[4 * PIECE : 4 * PIECE + 16, :] = two_parts(total)


def heads_finish_kernel(place, near_ref, far_ref, *refs):
    whole = refs[-1]
    for core, part, near, side in PLACES:
        ref = far_ref if core else near_ref
        low = target_of(part, near, side) * PIECE + part * SUB
        whole[pl.ds(row_of(place[0], core, part, near, side), SUB), :] = ref[low : low + SUB, :]
    for index in range(4):
        refs[index][...] = whole[index * 192 : index * 192 + 192, :].astype(F32)
    total = one_part(near_ref, 4 * PIECE) + one_part(far_ref, 4 * PIECE)
    for index in range(7):
        refs[4 + index][...] = total[index : index + 1, :].reshape(D)
    refs[11][...] = total[7:8, 0:192].reshape(192)
    refs[12][...] = total[7:8, 256:448].reshape(192)


def finish_kernel(which, place, near_ref, far_ref, out_ref, *scratch):
    whole = scratch[0] if scratch else out_ref
    for core, part, near, side in PLACES:
        block = (far_ref if core else near_ref)[part * 2 + near, which, side * SUB : (side + 1) * SUB, :]
        whole[pl.ds(row_of(place[0], core, part, near, side), SUB), :] = block.astype(whole.dtype)
    if scratch:
        out_ref[...] = whole[...].T.astype(F32)


def small_pack_kernel(place, in_ref, mid_ref, own_ref, near_ref, head0, head1, head2, head3, out_ref, column_ref):
    column_ref[...] = jnp.zeros(column_ref.shape, F32)
    for shard in range(4):
        for index, spot in enumerate(PLACES[:8]):
            ref, at = (own_ref, index) if shard == 0 else (near_ref, index // 2 * 6 + (shard - 1) * 2 + spot[3])
            column_ref[pl.ds(row_of(place[0], *spot), SUB), shard : shard + 1] = ref[:, at : at + 1]
    for shard, ref in enumerate((head0, head1, head2, head3)):
        for index in range(8):
            low = index // 4 * 256 + index % 4 * SUB
            column_ref[low : low + SUB, 4 + shard : 5 + shard] = ref[:, 16 + index : 17 + index]
    out_ref[0:2, :] = in_ref[...]
    out_ref[2:6, :] = mid_ref[...]
    out_ref[6:14, :] = column_ref[...].T[0:8, :]
    out_ref[14:16, :] = jnp.zeros((2, D), F32)


def shards(dp_size, z_size, tokens, cotangent, patch_count, word_mask, norm1_gain, norm1_shift, query_weight,
           query_bias, key_weight, value_weight, value_bias, out_weight, out_bias, norm2_gain, norm2_shift,
           up_weight, up_bias, down_weight, down_bias):
    rows = tokens.shape[0]
    place = jnp.stack([lax.axis_index("dp") % BLOCK, lax.axis_index("tensor")]).astype(jnp.int32)
    groups = [list(range(i, dp_size, BLOCK)) for i in range(BLOCK)]
    call = Chain()

    def swap(value, bit):
        return lax.ppermute(call.tie(value), "dp", [(i, i ^ bit) for i in range(dp_size)])

    def swap_z(value, bit):
        return lax.ppermute(call.tie(value), "tensor", [(i, i ^ bit) for i in range(z_size)])

    heads = query_weight.T, key_weight.T, value_weight.T, out_weight
    low = place[0] % 2 * PIECE
    heads_piece = lax.select_n(place[0] // 2, *[lax.dynamic_slice(value, (low, 0), (PIECE, D)) for value in heads])
    heads_at = [swap_z(heads_piece, bit) for bit in (1, 2, 3)]
    grad_got = swap(cotangent, 1)
    call.last = heads_piece
    bias, shift = call(
        small_prep_kernel, (flat(SUB, 128), flat(SLOTS, 8)), place,
        jnp.concatenate([word_mask, patch_count[:, None]], axis=1), jnp.concatenate([up_bias, query_bias, value_bias]),
        scratch=[flat(D + 384, 8), flat(8, SLOTS)])
    bias1 = swap_z(bias, 1)
    up_order, piece = call(functools.partial(hidden_prep_kernel, 0), (half(D, D), half(2, PIECE, D)), place, up_weight,
                           scratch=[half(D, D)])
    down_order, piece = call(functools.partial(hidden_prep_kernel, 1), (half(D, D), half(2, PIECE, D)), place,
                             down_weight, piece)
    grads = call(join_kernel, half(2 * rows, D), place, cotangent, grad_got)
    bias_pair = call(pack_kernel, flat(2, SUB, 128), place, bias, bias1)
    bias23 = swap_z(bias_pair, 2)
    h1 = call(norm1_kernel, half(rows, D), place, tokens, norm1_gain, norm1_shift)

    heads_at[0] = lax.optimization_barrier((heads_at[0], bias23))[0]
    mine = call(pack_kernel, half(3, PIECE, D), place, *heads_at)
    heads_near = [mine] + [swap(mine, bit) for bit in (2, 4, 6)]
    pieces = [swap_z(piece, bit) for bit in (1, 2)]
    heads_own = call(heads_prep_kernel, half(D, D), place, *heads)
    parts = [attend(call, 0, place, shift, h1, bias, [heads_own])]
    pieces.append(swap_z(pieces[1], 1))
    heads_near = call(pack_heads_kernel, half(3, 4, PIECE, D), place, *heads_near)
    halves = call(split_kernel, (half(3, SUB, D),) * 4, place, *pieces)
    heads_far = swap(heads_near, 1)
    halves = list(zip(halves, [swap(value, bit) for value, bit in zip(halves, (2, 4, 2, 4))]))

    def ahead(first, second):
        return call(ahead_kernel, (half(2, 3, SUB, D),) * 2, place, *first, *second)

    def across(first, second):
        return first, swap(first, 4), second, swap(second, 2)

    parts.append(attend(call, 1, place, shift, h1, bias1, [heads_near, heads_far]))
    parts.append(attend(call, 2, place, shift, h1, bias23[0], [heads_near, heads_far]))
    up_near = ahead(*halves[:2])
    down_near = ahead(*halves[2:])
    up_near = across(*up_near)
    down_near = across(*down_near)
    parts.append(attend(call, 3, place, shift, h1, bias23[1], [heads_near, heads_far]))
    weight, project, context, lse = zip(*parts)
    middle, h2, h2_first, h2_second = call(
        middle_kernel, (flat(rows, D), half(rows, D), half(rows // 2, D), half(rows // 2, D)), place, tokens, out_bias,
        norm2_gain, norm2_shift, *context, *weight)
    up_weight_near = call(pack_hidden_kernel, half(1152, D), place, *up_near)
    h2_first, h2_second = swap(h2_first, 1), swap(h2_second, 1)

    def units(count):
        return half(count, 2 * rows), half(count, 2 * rows)

    h2_all = call(join_kernel, half(2 * rows, D), place, h2, h2_first, h2_second)
    act0, slope0, *before = call(
        functools.partial(up_kernel, True), (*units(D // 2), *sends(1)), place, h2_all, grads, up_order, bias, bias23)
    act1, slope1, *down_sum = call(
        functools.partial(up_kernel, False), (*units(1152), *sends(4)), place, h2_all, grads, up_weight_near, bias1,
        bias23, *before)
    down_weight_near = call(pack_hidden_kernel, half(1152, D), place, *down_near)

    def to_plane(to_x, to_y, stay):
        return stay, swap(to_x, 2), swap(to_y, 4)

    def plane_sums(state):
        return call(plane_add_kernel, (half(2, 2, PIECE, D), half(2, 2, PIECE, D)), place, *state)

    def z_sums(stay, got):
        return call(z_add_kernel, (half(2, PIECE, D), half(2, PIECE, D)), place, stay, got)

    down_sum = to_plane(*down_sum)
    dpre0, sums0, *before = call(
        functools.partial(down_kernel, True), (half(D // 2, 2 * rows), flat(SUB, 128), *sends(1)), place, h2_all,
        grads, slope0, down_order)
    dpre1, sums1, *up_sum = call(
        functools.partial(down_kernel, False), (half(1152, 2 * rows), flat(SUB, 128), *sends(4)), place, h2_all,
        grads, slope1, down_weight_near, *before)
    ups = dpre0, dpre1, up_order, up_weight_near
    dh2 = call(functools.partial(partner_kernel, 2), (half(rows // 2, D),) * 2, place, *ups)
    dh2 = [swap(value, 1) for value in dh2]
    dmid, dmid_b, mid_sums = call(
        norm2_back_kernel, (flat(rows, D), half(rows, D), flat(4, D)), place, middle, cotangent, norm2_gain, *ups, *dh2)

    def attention_back(t):
        return attend_back(call, place, shift, dmid_b, h1, project[t], context[t], lse[t], weight[t])

    stay, go = plane_sums(down_sum)
    down_z = stay, swap_z(go, 1)
    up_sum = to_plane(*up_sum)
    back = {1: attention_back(1)}
    got = {1: swap(back[1][2], 1)}
    back[3] = attention_back(3)
    got[3] = swap(back[3][2], 1)
    back[2] = attention_back(2)
    back[0] = attention_back(0)
    stay, go = plane_sums(up_sum)
    down_go, down_stay = z_sums(*down_z)
    odd = call(functools.partial(heads_core_kernel, (0, 1)), (half(2, PIECE, D),) * 4, place, back[1][3], back[3][3],
               got[1], got[3])
    got[2], got[0] = swap(back[2][2], 1), swap(back[0][2], 1)
    up_z = stay, swap_z(go, 1)
    down_z = down_stay, swap_z(down_go, 2)
    heads_own_sum, to_x, to_y, to_xy = call(
        functools.partial(heads_core_kernel, (0, 2)), (half(4, PIECE, D),) * 4, place, back[0][3], back[2][3], got[0],
        got[2], *odd)
    heads_plane = [heads_own_sum, swap(to_x, 2), swap(to_y, 4), swap(to_xy, 6)]
    dproject, head_sums = zip(*[back[t][:2] for t in range(4)])
    input_grad, in_sums = call(norm1_back_kernel, (flat(rows, D), flat(2, D)), place, tokens, dmid, norm1_gain,
                               *dproject, *weight)
    small = call(small_pack_kernel, flat(16, D), place, in_sums, mid_sums, sums0, sums1, *head_sums,
                 scratch=[flat(D, 8)])
    downs = act0, act1, down_order, down_weight_near
    out_send = call(functools.partial(partner_kernel, 1), (half(rows, D),), place, *downs)[0]
    go, stay = z_sums(*up_z)
    up_z = stay, swap_z(go, 2)
    down_last = call(last_z_kernel, half(2, PIECE, D), place, *down_z)
    parts = call(heads_plane_kernel, (half(PIECE + 16, D),) * 4, place, *heads_plane, small)
    heads_z = [parts[0]] + [swap_z(parts[bit], bit) for bit in (1, 2, 3)]
    first, second = call(last_z_kernel, (half(2, PIECE, D),) * 2, place, *up_z, down_last)
    first_got, second_got = swap(first, 4), swap(second, 2)
    first, second = call(turned_kernel, (half(2, PIECE, D),) * 2, place, first, first_got, second, second_got)
    if dp_size > BLOCK:
        first, second = lax.psum((first, second), "dp", axis_index_groups=groups)
    mlp_last = [first, swap(first, 2), second, swap(second, 4)]
    mine = call(heads_z_kernel, half(PIECE + 16, D), place, *heads_z)
    if dp_size > BLOCK:
        mine = lax.psum(mine, "dp", axis_index_groups=groups)
    mlp_last = call(pack_kernel, half(4, 2, PIECE, D), place, *mlp_last)
    heads_last = [mine] + [swap(mine, bit) for bit in (2, 4, 6)]
    mlp_last_far = swap(mlp_last, 1)
    out_got = swap(out_send, 1)
    down_weight_grad = call(functools.partial(finish_kernel, 0), flat(D, D), place, mlp_last, mlp_last_far)
    layer_out = call(layer_out_kernel, half(rows, D), place, middle, down_bias, *downs, out_got)
    up_weight_grad = call(functools.partial(finish_kernel, 1), flat(D, D), place, mlp_last, mlp_last_far,
                          scratch=[half(D, D)])
    heads_last = call(heads_pack_kernel, half(4 * PIECE + 16, D), place, *heads_last)
    heads_last_far = swap(heads_last, 1)
    query_grad, key_grad, value_grad, out_weight_grad, *vectors = call(
        heads_finish_kernel, (flat(192, D),) * 4 + (flat(D),) * 7 + (flat(192),) * 2, place, heads_last,
        heads_last_far, scratch=[half(D, D)])
    return (
        layer_out, input_grad, vectors[0], vectors[1], query_grad.T, vectors[7], key_grad.T, value_grad.T, vectors[8],
        out_weight_grad, vectors[2], vectors[3], vectors[4], up_weight_grad, vectors[6], down_weight_grad, vectors[5],
    )


def solution(mesh):
    rows = P(("dp", "tensor"), None)
    columns = P(None, "tensor")
    part = P("tensor")
    part_rows = P("tensor", None)
    whole = P()
    return jax.shard_map(
        functools.partial(shards, mesh.shape["dp"], mesh.shape["tensor"]),
        mesh=mesh,
        in_specs=(rows, rows, P("dp"), P("dp", None), whole, whole, columns, part, columns, columns, part,
                  part_rows, whole, whole, whole, columns, part, part_rows, whole),
        out_specs=(rows, rows, whole, whole, columns, part, columns, columns, part, part_rows, whole, whole,
                   whole, columns, part, part_rows, whole),
        check_vma=False,
    )
```

```python
import functools
import math

import jax
import jax.numpy as jnp
from jax import lax
from jax.experimental import pallas as pl
from jax.experimental.pallas import tpu as pltpu
from jax.sharding import PartitionSpec as P

D = 768
HEAD_DIM = 64
HEADS_OWN = 3
ITEMS_OWN = 2
WORDS = 40
SLOTS = 256
NORM_EPS = 1e-05
MASKED = -1e30
BLOCK = 8
PIECE = D // BLOCK
SUB = PIECE // 2
F32 = jnp.float32
BF16 = jnp.bfloat16
STACK = 6 * 1024 * 1024


def nn(left, right):
    return lax.dot_general(left, right, (((1,), (0,)), ((), ())), preferred_element_type=F32)


def nt(left, right):
    return lax.dot_general(left, right, (((1,), (1,)), ((), ())), preferred_element_type=F32)


def tn(left, right):
    return lax.dot_general(left, right, (((0,), (0,)), ((), ())), preferred_element_type=F32)


def norm_stats(values):
    mean = jnp.mean(values, axis=-1, keepdims=True)
    centered = values - mean
    factor = lax.rsqrt(jnp.mean(centered * centered, axis=-1, keepdims=True) + NORM_EPS)
    return centered * factor, factor


def norm_back(normed, factor, gain, grad):
    scaled = grad * gain
    mean_scaled = jnp.mean(scaled, axis=-1, keepdims=True)
    mean_product = jnp.mean(scaled * normed, axis=-1, keepdims=True)
    return factor * (scaled - mean_scaled - normed * mean_product)


def column_sum(values):
    return jnp.sum(values, axis=0, keepdims=True)


def row_sum(values):
    return jnp.sum(values, axis=1, keepdims=True)


def flat(*size):
    return jax.ShapeDtypeStruct(size, F32)


def half(*size):
    return jax.ShapeDtypeStruct(size, BF16)


def size_of(shape, dtype):
    shape = (1,) * (2 - len(shape)) + tuple(shape)
    return math.prod(shape[:-2]) * -(-shape[-2] // 8) * 8 * -(-shape[-1] // 128) * 128 * jnp.dtype(dtype).itemsize


class Chain:
    def __init__(self):
        self.last = None

    def tie(self, value):
        return value if self.last is None else lax.optimization_barrier((value, self.last))[0]

    def __call__(self, body, outs, *args, scratch=(), scalars=1):
        args = args[:scalars] + (self.tie(args[scalars]),) + args[scalars + 1 :]
        got = kernel(body, outs, *args, scratch=scratch, scalars=scalars)
        self.last = jax.tree.leaves(got)[-1]
        return got


def kernel(body, outs, *args, scratch=(), scalars=1):
    held = list(args[scalars:]) + jax.tree.leaves(outs) + list(scratch)
    limit = STACK + sum(size_of(h.shape, h.dtype) for h in held)
    return pl.pallas_call(
        body,
        name=(body.func if isinstance(body, functools.partial) else body).__name__,
        out_shape=outs,
        in_specs=[pl.BlockSpec(memory_space=pltpu.SMEM)] * scalars
        + [pl.BlockSpec(memory_space=pltpu.VMEM)] * (len(args) - scalars),
        out_specs=jax.tree.map(lambda _: pl.BlockSpec(memory_space=pltpu.VMEM), outs),
        scratch_shapes=[pltpu.VMEM(s.shape, s.dtype) for s in scratch],
        compiler_params=pltpu.CompilerParams(vmem_limit_bytes=limit),
        cost_estimate=pl.CostEstimate(flops=1, bytes_accessed=1, transcendentals=1),
    )(*args)


def line(ref):
    return ref[...].reshape(1, -1)


def row_of(me, core, part, near, side):
    mine, x, y = me & 1, (me >> 1) & 1, me >> 2
    ahead, beside = (x, y) if part == 0 else (y, x)
    row = part * (D // 2) + ((ahead ^ near) * 2 + (mine ^ core)) * PIECE + (beside ^ side) * SUB
    return pl.multiple_of(row, 16)


PLACES = [(core, part, near, side) for core in (0, 1) for part in (0, 1) for near in (0, 1) for side in (0, 1)]


def heads_prep_kernel(place, query_ref, key_ref, value_ref, out_ref, whole_ref):
    for index, ref in enumerate((query_ref, key_ref, value_ref, out_ref)):
        whole_ref[index * 192 : index * 192 + 192, :] = ref[...]


def hidden_prep_kernel(which, place, weight_ref, *refs):
    if which == 0:
        order_ref, piece_ref, scratch = refs
        scratch[...] = weight_ref[...].T
        weight_ref = scratch
    else:
        before_ref, order_ref, piece_ref = refs
        piece_ref[0] = before_ref[0]
    for index, (core, part, near, side) in enumerate(PLACES):
        block = weight_ref[pl.ds(row_of(place[0], core, part, near, side), SUB), :]
        order_ref[index * SUB : (index + 1) * SUB, :] = block
        if core + near + side == 0:
            piece_ref[which, part * SUB : (part + 1) * SUB, :] = block


def small_prep_kernel(place, keys_ref, vectors_ref, bias_ref, shift_ref, column_ref, rows_ref):
    bias_ref[...] = jnp.zeros(bias_ref.shape, F32)
    size = vectors_ref.shape[0]
    column_ref[...] = jnp.broadcast_to(line(vectors_ref), (8, size)).T
    for index, spot in enumerate(PLACES):
        bias_ref[:, index : index + 1] = column_ref[pl.ds(row_of(place[0], *spot), SUB), 0:1]
    for index in range(8):
        low = D + index * SUB
        bias_ref[:, 16 + index : 17 + index] = column_ref[low : low + SUB, 0:1]
    lane = lax.broadcasted_iota(jnp.int32, (1, SLOTS), 1)
    rows_ref[...] = jnp.zeros(rows_ref.shape, F32)
    for item in range(ITEMS_OWN):
        row = keys_ref[pl.ds(place[1] * ITEMS_OWN + item, 1), :]
        count = row[:, WORDS : WORDS + 1]
        rows_ref[item : item + 1, 0:WORDS] = row[:, 0:WORDS].astype(F32)
        live = jnp.where(lane < WORDS, rows_ref[item : item + 1, :], jnp.where(lane - WORDS < count, 1.0, 0.0))
        rows_ref[item : item + 1, :] = jnp.where(live > 0, 0.0, MASKED)
    shift_ref[...] = rows_ref[...].T


def join_kernel(place, *refs):
    low = 0
    for ref in refs[:-1]:
        refs[-1][low : low + ref.shape[0], :] = ref[...]
        low += ref.shape[0]


def pack_kernel(place, *refs):
    for index, ref in enumerate(refs[:-1]):
        refs[-1][index] = ref[...]


def pack_heads_kernel(place, *refs):
    for index, ref in enumerate(refs[:-1]):
        refs[-1][:, index] = ref[...]


def split_kernel(place, *refs):
    for shard in range(3):
        for kind in range(2):
            for part in range(2):
                refs[3 + part][kind, shard] = refs[shard][kind, part * SUB : (part + 1) * SUB, :]


def ahead_kernel(place, first, first_got, second, second_got, *outs):
    for part, (own, got) in enumerate(((first, first_got), (second, second_got))):
        for kind in range(2):
            outs[2 * kind + part][0] = own[kind]
            outs[2 * kind + part][1] = got[kind]


def pack_hidden(sources, weight_ref):
    for part in range(2):
        for side in range(2):
            for near in range(2):
                for shard in range(3):
                    row = (part * 2 + near) * 288 + shard * PIECE + side * SUB
                    weight_ref[row : row + SUB, :] = sources[2 * part + side][near, shard]


def norm1_kernel(place, tokens_ref, gain_ref, shift_ref, h1_ref):
    normed, _ = norm_stats(tokens_ref[...].astype(F32))
    h1_ref[...] = (normed * line(gain_ref) + line(shift_ref)).astype(BF16)


def attend_kernel(shard, place, shift_ref, h1_ref, bias_ref, *refs):
    if shard == 0:
        weight_ref, project_ref, context_ref, lse_ref = refs
    else:
        near_ref, far_ref, weight_ref, project_ref, context_ref, lse_ref = refs
        for slot in range(BLOCK):
            ref = far_ref if slot % 2 else near_ref
            weight_ref[pl.ds(pl.multiple_of((place[0] ^ slot) * PIECE, 16), PIECE), :] = ref[shard - 1, slot // 2]
    h1 = h1_ref[...]
    bias = bias_ref[...]
    zero = jnp.zeros((192, 1), F32)
    columns = [jnp.concatenate([bias[:, at : at + 1] for at in range(first, first + 4)], axis=0) for first in (16, 20)]
    values = nt(weight_ref[0:576, :], h1) + jnp.concatenate([columns[0], zero, columns[1]], axis=0)
    project_ref[0:192, :] = (values[0:192] * HEAD_DIM**-0.5).astype(BF16)
    project_ref[192:576, :] = values[192:576].astype(BF16)
    for item in range(h1.shape[0] // SLOTS):
        columns = slice(item * SLOTS, item * SLOTS + SLOTS)
        shift = shift_ref[:, item : item + 1]
        for head in range(HEADS_OWN):
            query, key, value = (
                project_ref[part * 192 + head * 64 : part * 192 + head * 64 + 64, columns] for part in range(3)
            )
            scores = tn(key, query) + shift
            top = jnp.max(scores, axis=0, keepdims=True)
            exps = jnp.exp(scores - top)
            total = jnp.sum(exps, axis=0, keepdims=True)
            probs = (exps * (1.0 / total)).astype(BF16)
            lse_ref[item * HEADS_OWN + head : item * HEADS_OWN + head + 1, :] = top + jnp.log(total)
            context_ref[head * 64 : head * 64 + 64, columns] = nn(value, probs).astype(BF16)


def attend(call, shard, place, shift, h1, bias, weights):
    rows = h1.shape[0]
    outs = (half(576, rows), half(192, rows), flat(HEADS_OWN * rows // SLOTS, SLOTS))
    if shard:
        outs = (half(D, D),) + outs
    got = call(functools.partial(attend_kernel, shard), outs, place, shift, h1, bias, *weights)
    return got if shard else (weights[0], *got)


def middle_kernel(place, tokens_ref, out_bias_ref, gain_ref, shift_ref, *refs):
    contexts, weights, (middle_ref, h2_ref, first_ref, second_ref) = refs[:4], refs[4:8], refs[8:]
    total = tokens_ref[...].astype(F32) + line(out_bias_ref)
    context = jnp.concatenate([ref[...] for ref in contexts], axis=0)
    weight = jnp.concatenate([ref[576:768, :] for ref in weights], axis=0)
    total = total + tn(context, weight)
    middle_ref[...] = total
    normed, _ = norm_stats(total)
    h2 = (normed * line(gain_ref) + line(shift_ref)).astype(BF16)
    h2_ref[...] = h2
    first_ref[...] = h2[: h2.shape[0] // 2]
    second_ref[...] = h2[h2.shape[0] // 2 :]


def target_of(part, near, side):
    return near + 2 * side if part == 0 else side + 2 * near


def attend_back_kernel(place, shift_ref, dmid_ref, h1_ref, project_ref, context_ref, lse_ref, weight_ref, *refs):
    dproject_ref, sums_ref, send_ref, keep_ref, whole = refs
    dmid = dmid_ref[...]
    dcontext = nt(weight_ref[576:768, :], dmid).astype(BF16)
    for item in range(dmid.shape[0] // SLOTS):
        columns = slice(item * SLOTS, item * SLOTS + SLOTS)
        shift = shift_ref[:, item : item + 1]
        for head in range(HEADS_OWN):
            query, key, value = (
                project_ref[part * 192 + head * 64 : part * 192 + head * 64 + 64, columns] for part in range(3)
            )
            low = head * 64
            dctx = dcontext[low : low + 64, columns]
            lse = lse_ref[item * HEADS_OWN + head : item * HEADS_OWN + head + 1, :]
            delta = column_sum(dctx.astype(F32) * context_ref[low : low + 64, columns].astype(F32))
            probs = jnp.exp(tn(key, query) + (shift - lse))
            dscores = (probs * (tn(value, dctx) - delta)).astype(BF16)
            dproject_ref[low : low + 64, columns] = (nn(key, dscores) * HEAD_DIM**-0.5).astype(BF16)
            dproject_ref[192 + low : 256 + low, columns] = nt(query, dscores).astype(BF16)
            dproject_ref[384 + low : 448 + low, columns] = nt(dctx, probs.astype(BF16)).astype(BF16)
    sums_ref[...] = jnp.zeros(sums_ref.shape, F32)
    for which in (0, 2):
        total = row_sum(dproject_ref[which * 192 : which * 192 + 192, :].astype(F32))
        for i in range(4):
            at = 16 + which * 2 + i
            sums_ref[:, at : at + 1] = total[i * SUB : (i + 1) * SUB, :]
    whole[0:576, :] = nn(dproject_ref[...], h1_ref[...]).astype(BF16)
    whole[576:768, :] = nn(context_ref[...], dmid).astype(BF16)
    for core, part, near, side in PLACES:
        ref = send_ref if core else keep_ref
        ref[target_of(part, near, side), part * SUB : (part + 1) * SUB, :] = whole[
            pl.ds(row_of(place[0], core, part, near, side), SUB), :]


def attend_back(call, place, shift, dmid, h1, project, context, lse, weight):
    rows = h1.shape[0]
    outs = (half(576, rows), flat(SUB, 128), half(4, PIECE, D), half(4, PIECE, D))
    return call(attend_back_kernel, outs, place, shift, dmid, h1, project, context, lse, weight, scratch=[half(D, D)])


def norm1_back_kernel(place, tokens_ref, dmid_ref, gain_ref, *refs):
    grads, weights, (out_ref, sums_ref) = refs[:4], refs[4:8], refs[8:]
    total = tn(grads[0][...], weights[0][0:576, :])
    for grad_ref, weight_ref in zip(grads[1:], weights[1:]):
        total = total + tn(grad_ref[...], weight_ref[0:576, :])
    normed, factor = norm_stats(tokens_ref[...].astype(F32))
    out_ref[...] = dmid_ref[...] + norm_back(normed, factor, line(gain_ref), total)
    sums_ref[0:1, :] = column_sum(total * normed)
    sums_ref[1:2, :] = column_sum(total)


def bias_columns(biases, groups):
    return jnp.concatenate(
        [bias[:, 2 * group + side : 2 * group + side + 1] for group in groups for bias in biases for side in (0, 1)],
        axis=0)


def blocks(own):
    return [(0, 1, 2, 3)] if own else [(0,), (1,), (2,), (3,)]


def deliver(group, shards, product, x_ref, y_ref, stay_ref):
    for at, shard in enumerate(shards):
        spot = ORDER.index(shard)
        if group % 2 == 0:
            stay_ref[spot, group // 2] = product[at]
        else:
            (x_ref if group == 1 else y_ref)[spot] = product[at]


def deliver_before(before, x_ref, y_ref, stay_ref):
    x_ref[0], y_ref[0], stay_ref[0] = before[0][0], before[1][0], before[2][0]


def up_kernel(own, place, h2_ref, grad_ref, bias_ref, bias23_ref, *refs):
    if own:
        weight_ref, first_ref, second_ref, act_ref, slope_ref, x_ref, y_ref, stay_ref, all_ref = refs
        join_kernel(place, h2_ref, first_ref, second_ref, all_ref)
        h2 = all_ref[...]
        biases, shards = [bias_ref[...]], (0,)
    else:
        sources, before, (act_ref, slope_ref, x_ref, y_ref, stay_ref, weight_ref) = refs[:4], refs[4:7], refs[7:]
        pack_hidden(sources, weight_ref)
        h2 = h2_ref[...]
        deliver_before(before, x_ref, y_ref, stay_ref)
        biases, shards = [bias_ref[...], bias23_ref[0], bias23_ref[1]], (1, 2, 3)
    size = len(shards) * PIECE
    for block in blocks(own):
        rows = slice(block[0] * size, (block[-1] + 1) * size)
        pre = nt(weight_ref[rows, :], h2) + bias_columns(biases, block)
        below = 0.5 * (1.0 + lax.erf(pre * (2.0**-0.5)))
        act = (pre * below).astype(BF16)
        act_ref[rows, :] = act
        slope_ref[rows, :] = (below + pre * (jnp.exp(-0.5 * pre * pre) * ((2.0 * jnp.pi) ** -0.5))).astype(BF16)
        product = nn(act, grad_ref[...]).astype(BF16).reshape(len(block), len(shards), PIECE, D)
        for at, group in enumerate(block):
            deliver(group, shards, product[at], x_ref, y_ref, stay_ref)


def down_kernel(own, place, h2_ref, grad_ref, slope_ref, *refs):
    if own:
        weight_ref, dpre_ref, sums_ref, x_ref, y_ref, stay_ref = refs
        shards = (0,)
    else:
        sources, before, (dpre_ref, sums_ref, x_ref, y_ref, stay_ref, weight_ref) = refs[:4], refs[4:7], refs[7:]
        pack_hidden(sources, weight_ref)
        deliver_before(before, x_ref, y_ref, stay_ref)
        shards = (1, 2, 3)
    size = len(shards) * PIECE
    sums_ref[...] = jnp.zeros(sums_ref.shape, F32)
    for block in blocks(own):
        rows = slice(block[0] * size, (block[-1] + 1) * size)
        dpre = (nt(weight_ref[rows, :], grad_ref[...]) * slope_ref[rows, :].astype(F32)).astype(BF16)
        dpre_ref[rows, :] = dpre
        total = row_sum(dpre.astype(F32))
        for i in range(len(block) * size // SUB):
            at = block[0] * (size // SUB) + i
            sums_ref[:, at : at + 1] = total[i * SUB : (i + 1) * SUB, :]
        product = nn(dpre, h2_ref[...]).astype(BF16).reshape(len(block), len(shards), PIECE, D)
        for at, group in enumerate(block):
            deliver(group, shards, product[at], x_ref, y_ref, stay_ref)


def sends(count):
    return half(count, PIECE, D), half(count, PIECE, D), half(count, 2, PIECE, D)


def partner_kernel(place, own_ref, near_ref, own_weight_ref, near_weight_ref, *outs):
    rows = own_ref.shape[1] // 2
    total = tn(own_ref[:, rows:], own_weight_ref[0 : D // 2, :]) + tn(near_ref[:, rows:], near_weight_ref[...])
    low = 0
    for ref in outs:
        ref[...] = total[low : low + ref.shape[0]].astype(BF16)
        low += ref.shape[0]


def own_rows(own_ref, near_ref, own_weight_ref, near_weight_ref):
    rows = own_ref.shape[1] // 2
    return tn(own_ref[:, :rows], own_weight_ref[0 : D // 2, :]) + tn(near_ref[:, :rows], near_weight_ref[...])


def joined(refs):
    return jnp.concatenate([ref[...] for ref in refs], axis=0).astype(F32)


def own_rows_kernel(place, own_ref, near_ref, own_weight_ref, near_weight_ref, out_ref):
    out_ref[...] = own_rows(own_ref, near_ref, own_weight_ref, near_weight_ref)


def norm2_back_kernel(place, middle_ref, grad_ref, gain_ref, own_ref, first_ref, second_ref, dmid_ref, rounded_ref,
                      sums_ref):
    total = own_ref[...] + joined((first_ref, second_ref))
    normed, factor = norm_stats(middle_ref[...])
    grad = grad_ref[...].astype(F32)
    dmid = grad + norm_back(normed, factor, line(gain_ref), total)
    rounded = dmid.astype(BF16)
    dmid_ref[...] = dmid
    rounded_ref[...] = rounded
    sums_ref[0:1, :] = column_sum(rounded.astype(F32))
    sums_ref[1:2, :] = column_sum(total * normed)
    sums_ref[2:3, :] = column_sum(total)
    sums_ref[3:4, :] = column_sum(grad)


def layer_out_kernel(place, middle_ref, bias_ref, own_ref, near_ref, own_weight_ref, near_weight_ref, *refs):
    total = own_rows(own_ref, near_ref, own_weight_ref, near_weight_ref) + joined(refs[:-1])
    refs[-1][...] = (total + middle_ref[...] + line(bias_ref)).astype(BF16)


ORDER = (0, 2, 1, 3)


def added(left, right):
    return (left.astype(F32) + right.astype(F32)).astype(BF16)


def plane_add_kernel(place, stay_ref, x_ref, y_ref, *outs):
    for spot in range(stay_ref.shape[0]):
        ref = outs[spot // 2]
        ref[spot % 2, 0] = added(stay_ref[spot, 0], x_ref[spot])
        ref[spot % 2, 1] = added(stay_ref[spot, 1], y_ref[spot])


def both_add_kernel(place, stay_ref, x_ref, y_ref, keep_ref, got_ref, keep_out, z_out, z2_out, stay_out):
    plane_add_kernel(place, stay_ref, x_ref, y_ref, keep_out, z_out)
    z_add_kernel(place, keep_ref, got_ref, z2_out, stay_out)


def z_add_kernel(place, keep_ref, got_ref, z_ref, stay_ref):
    stay_ref[...] = added(keep_ref[0], got_ref[0])
    z_ref[...] = added(keep_ref[1], got_ref[1])


def last_z_kernel(place, keep_ref, got_ref, *refs):
    if len(refs) == 1:
        refs[0][...] = added(keep_ref[...], got_ref[...])
    else:
        before_ref, outs = refs[0], refs[1:]
        for part in range(2):
            outs[part][0] = before_ref[part]
            outs[part][1] = added(keep_ref[part], got_ref[part])


def turned_kernel(place, first, first_got, second, second_got, first_ref, second_ref):
    for value, got, out in ((first, first_got, first_ref), (second, second_got, second_ref)):
        out[:, 0:SUB, :] = added(value[:, 0:SUB, :], got[:, SUB:PIECE, :])
        out[:, SUB:PIECE, :] = added(value[:, SUB:PIECE, :], got[:, 0:SUB, :])


def heads_core_kernel(held, place, *refs):
    outs = refs[-4:]
    for at, shard in enumerate(held):
        for target in range(4):
            outs[target][shard] = added(refs[at][target], refs[2 + at][target])
    for target, ref in enumerate(refs[4:-4]):
        outs[target][1] = ref[0]
        outs[target][3] = ref[1]


def sum_of(refs, index):
    total = refs[0][index].astype(F32)
    for ref in refs[1:]:
        total = total + ref[index].astype(F32)
    return total.astype(BF16)


def two_parts(rows):
    high = rows.astype(BF16).astype(F32)
    return jnp.concatenate([high, rows - high], axis=0).astype(BF16)


def one_part(ref, low):
    rows = ref[low : low + 16, :].astype(F32)
    return rows[0:8] + rows[8:16]


def heads_plane_kernel(place, own_ref, x_ref, y_ref, xy_ref, small_ref, *outs):
    small = small_ref[...]
    for shard in range(4):
        outs[shard][0:PIECE, :] = sum_of((own_ref, x_ref, y_ref, xy_ref), shard)
        rows = [small[0:6], small[6 + shard : 7 + shard], small[10 + shard : 11 + shard]]
        outs[shard][PIECE : PIECE + 16, :] = two_parts(jnp.concatenate(rows, axis=0))


def heads_z_kernel(place, *refs):
    out_ref = refs[4]
    out_ref[0:PIECE, :] = sum_of([ref.at[0:PIECE] for ref in refs[:4]], Ellipsis)
    total = one_part(refs[0], PIECE)
    for ref in refs[1:4]:
        total = total + one_part(ref, PIECE)
    out_ref[PIECE : PIECE + 16, :] = two_parts(total)


def heads_pack_kernel(place, *refs):
    out_ref = refs[4]
    total = one_part(refs[0], PIECE)
    for ref in refs[1:4]:
        total = total + one_part(ref, PIECE)
    for index, ref in enumerate(refs[:4]):
        out_ref[index * PIECE : (index + 1) * PIECE, :] = ref[0:PIECE, :]
    out_ref[4 * PIECE : 4 * PIECE + 16, :] = two_parts(total)


def heads_finish_kernel(place, near_ref, far_ref, *refs):
    whole = refs[-1]
    for core, part, near, side in PLACES:
        ref = far_ref if core else near_ref
        low = target_of(part, near, side) * PIECE + part * SUB
        whole[pl.ds(row_of(place[0], core, part, near, side), SUB), :] = ref[low : low + SUB, :]
    for index in range(4):
        refs[index][...] = whole[index * 192 : index * 192 + 192, :].astype(F32)
    total = one_part(near_ref, 4 * PIECE) + one_part(far_ref, 4 * PIECE)
    for index in range(7):
        refs[4 + index][...] = total[index : index + 1, :].reshape(D)
    refs[11][...] = total[7:8, 0:192].reshape(192)
    refs[12][...] = total[7:8, 256:448].reshape(192)


def finish_kernel(which, place, near_ref, far_ref, out_ref, *scratch):
    whole = scratch[0] if scratch else out_ref
    for core, part, near, side in PLACES:
        block = (far_ref if core else near_ref)[part * 2 + near, which, side * SUB : (side + 1) * SUB, :]
        whole[pl.ds(row_of(place[0], core, part, near, side), SUB), :] = block.astype(whole.dtype)
    if scratch:
        out_ref[...] = whole[...].T.astype(F32)


def small_pack_kernel(place, in_ref, mid_ref, own_ref, near_ref, head0, head1, head2, head3, out_ref, column_ref):
    column_ref[...] = jnp.zeros(column_ref.shape, F32)
    for shard in range(4):
        for index, spot in enumerate(PLACES[:8]):
            ref, at = (own_ref, index) if shard == 0 else (near_ref, index // 2 * 6 + (shard - 1) * 2 + spot[3])
            column_ref[pl.ds(row_of(place[0], *spot), SUB), shard : shard + 1] = ref[:, at : at + 1]
    for shard, ref in enumerate((head0, head1, head2, head3)):
        for index in range(8):
            low = index // 4 * 256 + index % 4 * SUB
            column_ref[low : low + SUB, 4 + shard : 5 + shard] = ref[:, 16 + index : 17 + index]
    out_ref[0:2, :] = in_ref[...]
    out_ref[2:6, :] = mid_ref[...]
    out_ref[6:14, :] = column_ref[...].T[0:8, :]
    out_ref[14:16, :] = jnp.zeros((2, D), F32)


def shards(dp_size, z_size, tokens, cotangent, patch_count, word_mask, norm1_gain, norm1_shift, query_weight,
           query_bias, key_weight, value_weight, value_bias, out_weight, out_bias, norm2_gain, norm2_shift,
           up_weight, up_bias, down_weight, down_bias):
    rows = tokens.shape[0]
    place = jnp.stack([lax.axis_index("dp") % BLOCK, lax.axis_index("tensor")]).astype(jnp.int32)
    groups = [list(range(i, dp_size, BLOCK)) for i in range(BLOCK)]
    call = Chain()

    def swap(value, bit):
        return lax.ppermute(call.tie(value), "dp", [(i, i ^ bit) for i in range(dp_size)])

    def swap_z(value, bit):
        return lax.ppermute(call.tie(value), "tensor", [(i, i ^ bit) for i in range(z_size)])

    heads = query_weight.T, key_weight.T, value_weight.T, out_weight
    low = place[0] % 2 * PIECE
    heads_piece = lax.select_n(place[0] // 2, *[lax.dynamic_slice(value, (low, 0), (PIECE, D)) for value in heads])
    heads_at = [swap_z(heads_piece, bit) for bit in (1, 2, 3)]
    grad_got = swap(cotangent, 1)
    call.last = heads_piece
    bias, shift = call(
        small_prep_kernel, (flat(SUB, 128), flat(SLOTS, 8)), place,
        jnp.concatenate([word_mask, patch_count[:, None]], axis=1), jnp.concatenate([up_bias, query_bias, value_bias]),
        scratch=[flat(D + 384, 8), flat(8, SLOTS)])
    bias1 = swap_z(bias, 1)
    up_order, piece = call(functools.partial(hidden_prep_kernel, 0), (half(D, D), half(2, PIECE, D)), place, up_weight,
                           scratch=[half(D, D)])
    down_order, piece = call(functools.partial(hidden_prep_kernel, 1), (half(D, D), half(2, PIECE, D)), place,
                             down_weight, piece)
    grads = call(join_kernel, half(2 * rows, D), place, cotangent, grad_got)
    bias_pair = call(pack_kernel, flat(2, SUB, 128), place, bias, bias1)
    bias23 = swap_z(bias_pair, 2)
    h1 = call(norm1_kernel, half(rows, D), place, tokens, norm1_gain, norm1_shift)

    heads_at[0] = lax.optimization_barrier((heads_at[0], bias23))[0]
    mine = call(pack_kernel, half(3, PIECE, D), place, *heads_at)
    heads_near = [mine] + [swap(mine, bit) for bit in (2, 4, 6)]
    pieces = [swap_z(piece, bit) for bit in (1, 2)]
    heads_own = call(heads_prep_kernel, half(D, D), place, *heads)
    parts = [attend(call, 0, place, shift, h1, bias, [heads_own])]
    pieces.append(swap_z(pieces[1], 1))
    heads_near = call(pack_heads_kernel, half(3, 4, PIECE, D), place, *heads_near)
    first, second = call(split_kernel, (half(2, 3, SUB, D),) * 2, place, *pieces)
    heads_far = swap(heads_near, 1)
    halves = first, swap(first, 2), second, swap(second, 4)

    def across(first, second):
        return first, swap(first, 4), second, swap(second, 2)

    parts.append(attend(call, 1, place, shift, h1, bias1, [heads_near, heads_far]))
    parts.append(attend(call, 2, place, shift, h1, bias23[0], [heads_near, heads_far]))
    halves = call(ahead_kernel, (half(2, 3, SUB, D),) * 4, place, *halves)
    up_near = across(*halves[:2])
    down_near = across(*halves[2:])
    parts.append(attend(call, 3, place, shift, h1, bias23[1], [heads_near, heads_far]))
    weight, project, context, lse = zip(*parts)
    middle, h2, h2_first, h2_second = call(
        middle_kernel, (flat(rows, D), half(rows, D), half(rows // 2, D), half(rows // 2, D)), place, tokens, out_bias,
        norm2_gain, norm2_shift, *context, *weight)
    h2_first, h2_second = swap(h2_first, 1), swap(h2_second, 1)

    def units(count):
        return half(count, 2 * rows), half(count, 2 * rows)

    def to_plane(to_x, to_y, stay):
        return stay, swap(to_x, 2), swap(to_y, 4)

    h2, *up_near = lax.optimization_barrier((h2, *up_near))
    act0, slope0, *before, h2_all = call(
        functools.partial(up_kernel, True), (*units(D // 2), *sends(1), half(2 * rows, D)), place, h2, grads, bias,
        bias23, up_order, h2_first, h2_second)
    act1, slope1, *down_sum, up_weight_near = call(
        functools.partial(up_kernel, False), (*units(1152), *sends(4), half(1152, D)), place, h2_all, grads, bias1,
        bias23, *up_near, *before)
    down_sum[0], *down_near = lax.optimization_barrier((down_sum[0], *down_near))
    down_sum[1] = lax.optimization_barrier((down_sum[1], down_near[1], down_near[3]))[0]
    down_sum = to_plane(*down_sum)
    dpre0, sums0, *before = call(
        functools.partial(down_kernel, True), (half(D // 2, 2 * rows), flat(SUB, 128), *sends(1)), place, h2_all,
        grads, slope0, down_order)

    def plane_sums(state):
        return call(plane_add_kernel, (half(2, 2, PIECE, D), half(2, 2, PIECE, D)), place, *state)

    def z_sums(stay, got):
        return call(z_add_kernel, (half(2, PIECE, D), half(2, PIECE, D)), place, stay, got)

    dpre1, sums1, *up_sum, down_weight_near = call(
        functools.partial(down_kernel, False), (half(1152, 2 * rows), flat(SUB, 128), *sends(4), half(1152, D)), place,
        h2_all, grads, slope1, *down_near, *before)
    ups = dpre0, dpre1, up_order, up_weight_near
    dh2 = call(partner_kernel, (half(rows // 2, D),) * 2, place, *ups)
    dh2 = [swap(value, 1) for value in dh2]
    dh2.insert(0, call(own_rows_kernel, flat(rows, D), place, *ups))
    dmid, dmid_b, mid_sums = call(
        norm2_back_kernel, (flat(rows, D), half(rows, D), flat(4, D)), place, middle, cotangent, norm2_gain, *dh2)

    def attention_back(t):
        return attend_back(call, place, shift, dmid_b, h1, project[t], context[t], lse[t], weight[t])

    stay, go = plane_sums(down_sum)
    down_z = stay, swap_z(go, 1)
    up_sum = to_plane(*up_sum)
    back = {1: attention_back(1)}
    got = {1: swap(back[1][2], 1)}
    back[3] = attention_back(3)
    got[3] = swap(back[3][2], 1)
    back[2] = attention_back(2)
    back[0] = attention_back(0)
    stay, go, down_go, down_stay = call(
        both_add_kernel, (half(2, 2, PIECE, D),) * 2 + (half(2, PIECE, D),) * 2, place, *up_sum, *down_z)
    got[2], got[0] = swap(back[2][2], 1), swap(back[0][2], 1)
    up_z = stay, swap_z(go, 1)
    odd = call(functools.partial(heads_core_kernel, (0, 1)), (half(2, PIECE, D),) * 4, place, back[1][3], back[3][3],
               got[1], got[3])
    down_z = down_stay, swap_z(down_go, 2)
    heads_own_sum, to_x, to_y, to_xy = call(
        functools.partial(heads_core_kernel, (0, 2)), (half(4, PIECE, D),) * 4, place, back[0][3], back[2][3], got[0],
        got[2], *odd)
    heads_plane = [heads_own_sum, swap(to_x, 2), swap(to_y, 4), swap(to_xy, 6)]
    dproject, head_sums = zip(*[back[t][:2] for t in range(4)])
    input_grad, in_sums = call(norm1_back_kernel, (flat(rows, D), flat(2, D)), place, tokens, dmid, norm1_gain,
                               *dproject, *weight)
    small = call(small_pack_kernel, flat(16, D), place, in_sums, mid_sums, sums0, sums1, *head_sums,
                 scratch=[flat(D, 8)])
    downs = act0, act1, down_order, down_weight_near
    out_sends = call(partner_kernel, (half(rows // 4, D), half(3 * rows // 4, D)), place, *downs)
    go, stay = z_sums(*up_z)
    up_z = stay, swap_z(go, 2)
    down_last = call(last_z_kernel, half(2, PIECE, D), place, *down_z)
    parts = call(heads_plane_kernel, (half(PIECE + 16, D),) * 4, place, *heads_plane, small)
    heads_z = [parts[0]] + [swap_z(parts[bit], bit) for bit in (1, 2, 3)]
    first, second = call(last_z_kernel, (half(2, PIECE, D),) * 2, place, *up_z, down_last)
    first_got, second_got = swap(first, 4), swap(second, 2)
    first, second = call(turned_kernel, (half(2, PIECE, D),) * 2, place, first, first_got, second, second_got)
    if dp_size > BLOCK:
        first, second = lax.psum((first, second), "dp", axis_index_groups=groups)
    mlp_last = [first, swap(first, 2), second, swap(second, 4)]
    mine = call(heads_z_kernel, half(PIECE + 16, D), place, *heads_z)
    if dp_size > BLOCK:
        mine = lax.psum(mine, "dp", axis_index_groups=groups)
    out_gots = [swap(out_sends[0], 1)]
    mlp_last[0] = lax.optimization_barrier((mlp_last[0], out_gots[0]))[0]
    mlp_last = call(pack_kernel, half(4, 2, PIECE, D), place, *mlp_last)
    heads_last = [mine] + [swap(mine, bit) for bit in (2, 4, 6)]
    mlp_last_far = swap(mlp_last, 1)
    out_gots.append(swap(out_sends[1], 1))
    down_weight_grad = call(functools.partial(finish_kernel, 0), flat(D, D), place, mlp_last, mlp_last_far)
    layer_out = call(layer_out_kernel, half(rows, D), place, middle, down_bias, *downs, *out_gots)
    up_weight_grad = call(functools.partial(finish_kernel, 1), flat(D, D), place, mlp_last, mlp_last_far,
                          scratch=[half(D, D)])
    heads_last = call(heads_pack_kernel, half(4 * PIECE + 16, D), place, *heads_last)
    heads_last_far = swap(heads_last, 1)
    query_grad, key_grad, value_grad, out_weight_grad, *vectors = call(
        heads_finish_kernel, (flat(192, D),) * 4 + (flat(D),) * 7 + (flat(192),) * 2, place, heads_last,
        heads_last_far, scratch=[half(D, D)])
    return (
        layer_out, input_grad, vectors[0], vectors[1], query_grad.T, vectors[7], key_grad.T, value_grad.T, vectors[8],
        out_weight_grad, vectors[2], vectors[3], vectors[4], up_weight_grad, vectors[6], down_weight_grad, vectors[5],
    )


def solution(mesh):
    rows = P(("dp", "tensor"), None)
    columns = P(None, "tensor")
    part = P("tensor")
    part_rows = P("tensor", None)
    whole = P()
    return jax.shard_map(
        functools.partial(shards, mesh.shape["dp"], mesh.shape["tensor"]),
        mesh=mesh,
        in_specs=(rows, rows, P("dp"), P("dp", None), whole, whole, columns, part, columns, columns, part,
                  part_rows, whole, whole, whole, columns, part, part_rows, whole),
        out_specs=(rows, rows, whole, whole, columns, part, columns, columns, part, part_rows, whole, whole,
                   whole, columns, part, part_rows, whole),
        check_vma=False,
    )
```
